128 devices in a mesh: tm: 8 (over z, x_lo), space: 16 (over x_hi, y, core).
Axes of the slice: x: 4 (x_hi: 2, x_lo: 2; x = x_hi * 2 + x_lo), y: 4, z: 4, core: 2. Of those that a mesh axis runs over, the one named last changes fastest.
Arguments:
- start_states: float32 [8, 128, 16, 1024], P('tm', 'space'), may hold values from 0.2 to 2
- dispersion: float32 [128, 16, 1024], P('space'), may hold values from 0.02 to 0.12
- soil_class: int32 [128, 16, 1024], P('space'), may hold values from 0 to 11
- sorption_k: float32 [12], replicated, may hold values from 0.3 to 3
- sorption_n: float32 [12], replicated, may hold values from 0.6 to 1
Outputs:
- next_states: float32 [8, 128, 16, 1024], P('tm', 'space')
The draws below stay inside these ranges and needn't reach their ends.
All inputs are finite; a program needn't handle non-finite values.
Results may differ from the reference program's by a relative error of at most 0.0001.
Values sent between devices are 32-bit elements; how exact they have to be, the bound alone decides.
A program may use at most 256 MiB of HBM per device.

```python
import math
import jax
import jax.numpy as jnp

NZ = 16
NY = 1024
CLASSES = 12
FINE_STEPS = 4
COARSE_STEPS = 2
SLICES = 8
NX = 128


def touch_ends(values, rng, smallest, top_value):
    place = [jax.random.randint(jax.random.fold_in(rng, axis), (), 0, length) for axis, length in enumerate(values.shape)]
    longest = values.shape.index(max(values.shape))
    neighbour = place[:longest] + [(place[longest] + 1) % values.shape[longest]] + place[longest + 1:]
    return values.at[tuple(place)].set(smallest).at[tuple(neighbour)].set(top_value)


def block_levels(stream_key, shape, shards, low, largest):
    factor_of, own = 1.0, jax.random.fold_in(stream_key, 6)
    for dim, shards_of in shards:
        steps = jnp.exp(jax.random.uniform(jax.random.fold_in(own, dim), (shards_of,), jnp.float32, low / len(shards), largest / len(shards)))
        factor_of = factor_of * jnp.repeat(steps, shape[dim] // shards_of).reshape([-1 if axis == dim else 1 for axis in range(len(shape))])
    return factor_of


def setup_inputs(seed: int = 0) -> dict:
    streams_of = jax.random.split(jax.random.key(seed), 6)
    return {
        "start_states": jnp.clip(jnp.exp(math.log(2.0) - 2.3025851 * jax.random.uniform(streams_of[0], (SLICES, NX, NZ, NY), jnp.float32) ** block_levels(streams_of[0], (SLICES, NX, NZ, NY), ((0, 8), (1, 16)), -0.2, 0.2)), 0.2, 2.0),
        "dispersion": jnp.clip(0.02 + 0.09999999776482582 * jax.random.uniform(streams_of[1], (NX, NZ, NY), jnp.float32) ** block_levels(streams_of[1], (NX, NZ, NY), ((0, 16),), -0.2, 0.2), 0.02, 0.12),
        "soil_class": touch_ends(jax.random.randint(streams_of[2], (NX, NZ, NY), 0, CLASSES), jax.random.fold_in(streams_of[2], 1), 0, CLASSES - 1).astype(jnp.int32),
        "sorption_k": jnp.clip(jnp.exp(jax.random.uniform(streams_of[3], (CLASSES,), jnp.float32, math.log(0.3), math.log(3.0))), 0.3, 3.0),
        "sorption_n": jnp.clip(jax.random.uniform(streams_of[4], (CLASSES,), jnp.float32, 0.6, 1.0), 0.6, 1.0),
    }


speed_x = 0.3
speed_z = 0.2
density_ratio = 2.0


def advance(middle, west_rows, east_rows, spread_coef, k_field, n_field, step_size, spacing):
    z_padded = jnp.pad(middle, ((0, 0), (1, 1), (0, 0)))
    y_padded = jnp.pad(middle, ((0, 0), (0, 0), (1, 1)))
    laplace = west_rows + east_rows + z_padded[:, 2:] + z_padded[:, :-2] + y_padded[:, :, 2:] + y_padded[:, :, :-2] - 6.0 * middle
    upwind = speed_x * (middle - west_rows) + speed_z * (middle - z_padded[:, :-2])
    retard = 1.0 + density_ratio * k_field * n_field * jnp.exp((n_field - 1.0) * jnp.log(jnp.abs(middle) + 0.1))
    return middle + step_size * (spread_coef * laplace / (spacing * spacing) - upwind / spacing) / retard


def whole_step(field_now, spread_coef, k_field, n_field, step_size, spacing):
    padded = jnp.pad(field_now, ((1, 1), (0, 0), (0, 0)))
    return advance(field_now, padded[:-2], padded[2:], spread_coef, k_field, n_field, step_size, spacing)


def restrict(field_now):
    a, b, c = field_now.shape
    return field_now.reshape(a // 2, 2, b // 2, 2, c // 2, 2).mean(axis=(1, 3, 5))


def prolong(coarse):
    return jnp.repeat(jnp.repeat(jnp.repeat(coarse, 2, axis=0), 2, axis=1), 2, axis=2)


def reference(start_states, dispersion, soil_class, sorption_k, sorption_n):
    k_field = sorption_k[soil_class]
    n_field = sorption_n[soil_class]
    coarse_d = restrict(dispersion)
    coarse_k = restrict(k_field)
    coarse_n = restrict(n_field)

    def fine_run(field_now):
        for step in range(FINE_STEPS):
            field_now = whole_step(field_now, dispersion, k_field, n_field, 0.6, 1.0)
        return field_now

    def coarse_run(coarse):
        for step in range(COARSE_STEPS):
            coarse = whole_step(coarse, coarse_d, coarse_k, coarse_n, 1.2, 2.0)
        return coarse

    carried = restrict(start_states[0])
    results = []
    for slice_index in range(SLICES):
        fine_end = fine_run(start_states[slice_index])
        own_coarse = coarse_run(restrict(start_states[slice_index]))
        chain_coarse = coarse_run(carried)
        results.append(fine_end + prolong(chain_coarse - own_coarse))
        carried = chain_coarse + restrict(fine_end) - own_coarse
    return jnp.stack(results)
```

```python
import functools

import jax
import jax.numpy as jnp
from jax import lax
from jax.experimental import pallas as pl
from jax.experimental.pallas import tpu as pltpu
from jax.sharding import PartitionSpec as P

MESH = pl.DeviceIdType.MESH
F32 = jnp.float32

SPEED_X = 0.3
SPEED_Z = 0.2
DENSITY = 2.0

ROWS = 8
HALO = 4
EXT = ROWS + 2 * HALO
NZ = 16
NY = 1024
CROWS = 4
CZ = 8
CY = 512
SLICES = 8
SPACE = 16
GROUPS = 10
CHAIN_ROWS = GROUPS * CROWS
OWN = 16
LANES = 128

PIECES = (
    (0, 2, 2, 12),
    (1, 3, 1, 12),
    (2, 3, 1, 12),
    (0, 0, 2, 14),
    (1, 2, 1, 13),
    (2, 2, 1, 13),
    (1, 1, 1, 14),
    (2, 1, 1, 14),
)


def reach(tau):
    return (17 - 2 * tau) // 4


def shifted(c, axis, size, steps, index):
    rolled = pltpu.roll(c, steps % size, axis)
    return jnp.where(index == (0 if steps > 0 else size - 1), 0.0, rolled)


def update(c, w, e, zm, zp, ym, yp, d, a, m, scale, per_h):
    lap = ((w + e) + (zm + zp)) + ((ym + yp) - 6.0 * c)
    adv = (SPEED_X * per_h) * (c - w) + (SPEED_Z * per_h) * (c - zm)
    ret = 1.0 + a * jnp.exp(m * jnp.log(jnp.abs(c) + 0.1))
    return c + scale * ((d * lap - adv) / ret)


def main_kernel(
    k_ref, n_ref, start, disp, soil, fine_out, diff_out,
    u0, u1, u2, dx, cx, ax, mx, rc, rc1, own, dc, ac, mc, win, fwin,
    cbuf, fbuf, cw0, cw1, gout, gbuf,
    local_sem, halo_send, halo_recv, win_send, win_recv, f_send, f_recv, g_send, g_recv, out_sem,
):
    t = lax.axis_index("tm")
    s = lax.axis_index("space")
    chip = s // 2
    core = lax.rem(s, 2)
    even = core == 0
    is_first = s == 0
    is_last = s == SPACE - 1

    def clear(first):
        for ref in (u0, dx):
            ref[pl.ds(first, HALO)] = jnp.zeros((HALO, NZ, NY), F32)
        cx[pl.ds(first, HALO)] = jnp.zeros((HALO, NZ, NY), jnp.int32)

    barrier = pltpu.get_barrier_semaphore()

    def tell(tt, ss):
        pl.semaphore_signal(barrier, inc=1, device_id=(tt, ss), device_id_type=MESH)

    @pl.when(jnp.logical_not(is_first))
    def _():
        tell(t, s - 1)

    @pl.when(jnp.logical_not(is_last))
    def _():
        tell(t, s + 1)

    local = [
        pltpu.make_async_copy(src, dst.at[pl.ds(HALO, ROWS)], local_sem.at[i])
        for i, (src, dst) in enumerate(((start, u0), (disp, dx), (soil, cx)))
    ]
    for copy in local:
        copy.start()

    def tell_chain(i, carry):
        tt = i // GROUPS
        ss = 2 * chip - 4 + lax.rem(i, GROUPS)
        inside = (ss >= 0) & (ss < SPACE) & jnp.logical_not((tt == t) & (ss == s))

        @pl.when(inside & even)
        def _():
            tell(tt, ss)

        return carry

    lax.fori_loop(0, SLICES * GROUPS, tell_chain, 0)

    def tell_result(j, carry):
        @pl.when(jnp.logical_not((j == t) & even))
        def _():
            tell(j, 2 * chip)

        return carry

    lax.fori_loop(0, SLICES, tell_result, 0)

    @pl.when(is_first)
    def _():
        clear(0)

    @pl.when(is_last)
    def _():
        clear(HALO + ROWS)

    first_chip = jnp.maximum(chip - 2, 0)
    last_chip = jnp.minimum(chip + 2, SPACE // 2 - 1)
    near = 2 - is_first.astype(jnp.int32) - is_last.astype(jnp.int32)
    chain_peers = SLICES * (last_chip - first_chip + 1)
    pl.semaphore_wait(barrier, near + chain_peers + jnp.where(even, 2 * SLICES - 2, 0))

    sources = (start, disp, soil)
    targets = (u0, dx, cx)

    def halo_copy(index, side):
        array, low, count, high = PIECES[index]
        first = jnp.where(side == 0, low, high)
        origin = jnp.where(side == 0, low + HALO, high - HALO - ROWS)
        return pltpu.make_async_remote_copy(
            src_ref=sources[array].at[pl.ds(origin, count)],
            dst_ref=targets[array].at[pl.ds(first, count)],
            send_sem=halo_send.at[index, side],
            recv_sem=halo_recv.at[index, side],
            device_id=(t, jnp.where(side == 0, s + 1, s - 1)),
            device_id_type=MESH,
        )

    far_to = 1 - core
    far_side = core
    far_valid = jnp.logical_not(is_first | is_last)

    @pl.when(far_valid)
    def _():
        for index in range(len(PIECES)):
            halo_copy(index, far_to).start()

    for index in range(len(PIECES)):
        halo_copy(index, 1 - far_to).start()

    lane = lax.broadcasted_iota(jnp.int32, (8, LANES), 1)
    k_table = jnp.zeros((8, LANES), F32)
    n_table = jnp.zeros((8, LANES), F32)
    for i in range(k_ref.shape[0]):
        k_table = jnp.where(lane == i, k_ref[i], k_table)
        n_table = jnp.where(lane == i, n_ref[i], n_table)
    compact = lax.rem(2 * lane, LANES)
    zi = lax.broadcasted_iota(jnp.int32, (NZ, NY), 0)
    yi = lax.broadcasted_iota(jnp.int32, (NZ, NY), 1)
    czi = lax.broadcasted_iota(jnp.int32, (CZ, CY), 0)
    cyi = lax.broadcasted_iota(jnp.int32, (CZ, CY), 1)

    def take(value, index):
        return jnp.take_along_axis(value, index, axis=1)

    def look_up(row):
        k_parts, m_parts = [], []
        for z in range(0, NZ, 8):
            k_line, m_line = [], []
            for y in range(0, NY, LANES):
                soil_now = cx[row, z : z + 8, y : y + LANES]
                k = take(k_table, soil_now)
                n = take(n_table, soil_now)
                m = n - 1.0
                ax[row, z : z + 8, y : y + LANES] = (DENSITY * k) * n
                mx[row, z : z + 8, y : y + LANES] = m
                k_line.append(k)
                m_line.append(m)
            k_parts.append(jnp.concatenate(k_line, axis=1))
            m_parts.append(jnp.concatenate(m_line, axis=1))
        return jnp.concatenate(k_parts, axis=0), jnp.concatenate(m_parts, axis=0)

    sub = lax.broadcasted_iota(jnp.int32, (8, LANES), 0)
    compact_z = lax.rem(2 * sub, 8)

    def restrict(total):
        out = []
        for i in range(CY // LANES):
            halves = []
            for half in range(2):
                y = (2 * i + half) * LANES
                parts = []
                for z in range(0, NZ, 8):
                    value = total[z : z + 8, y : y + LANES]
                    value = value + pltpu.roll(value, 7, 0)
                    parts.append(jnp.take_along_axis(value, compact_z, axis=0))
                value = jnp.where(sub < 4, parts[0], parts[1])
                value = value + pltpu.roll(value, LANES - 1, 1)
                halves.append(take(value, compact))
            out.append(jnp.where(lane < LANES // 2, halves[0], halves[1]))
        return 0.125 * jnp.concatenate(out, axis=1)

    def fields(p):
        k_low, m_low = look_up(2 * p)
        k_high, m_high = look_up(2 * p + 1)
        coarse_k = restrict(k_low + k_high)
        coarse_m = restrict(m_low + m_high)
        dc[p] = restrict(dx[2 * p] + dx[2 * p + 1])
        ac[p] = (DENSITY * coarse_k) * (coarse_m + 1.0)
        mc[p] = coarse_m

    def restrict_start(p):
        rc[p] = restrict(u0[2 * p] + u0[2 * p + 1])

    def fine_row(src, dst, row):
        outside = (is_first & (row < HALO)) | (is_last & (row >= HALO + ROWS))
        c, w, e = src[row], src[row - 1], src[row + 1]
        dst[row] = update(
            c, w, e,
            shifted(c, 0, NZ, 1, zi), shifted(c, 0, NZ, -1, zi),
            shifted(c, 1, NY, 1, yi), shifted(c, 1, NY, -1, yi),
            dx[row], ax[row], mx[row], jnp.where(outside, 0.0, 0.6), 1.0,
        )

    def loop(first, last, function):
        def run(i, carry):
            function(i)
            return carry

        lax.fori_loop(first, last, run, 0)

    for copy in local:
        copy.wait()
    loop(2, 6, fields)
    loop(2, 6, restrict_start)
    loop(5, 11, functools.partial(fine_row, u0, u1))
    loop(6, 10, functools.partial(fine_row, u1, u2))
    loop(7, 9, functools.partial(fine_row, u2, u1))

    def diagonal(side, d):
        for k, (src, dst) in enumerate(((u0, u1), (u1, u2), (u2, u1), (u1, u2))):
            low = HALO - d + k
            fine_row(src, dst, jnp.where(side == 0, low, EXT - 1 - low))

    def arrive(side, valid, *indices):
        @pl.when(valid)
        def _():
            for index in indices:
                halo_copy(index, side).wait_recv()

    def pair_of(side, p):
        return jnp.where(side == 0, p, EXT // 2 - 1 - p)

    def work_side(side, valid, between):
        arrive(side, valid, 0)
        diagonal(side, 0)
        restrict_start(pair_of(side, 1))
        arrive(side, valid, 1, 2)
        look_up(jnp.where(side == 0, 3, 12))
        diagonal(side, 1)
        arrive(side, valid, 3, 4, 5)
        fields(pair_of(side, 1))
        diagonal(side, 2)
        restrict_start(pair_of(side, 0))
        between()
        arrive(side, valid, 6, 7)
        look_up(jnp.where(side == 0, 1, 14))
        diagonal(side, 3)

    def windows(value):
        tiles = [value[:, i * LANES : (i + 1) * LANES] for i in range(CY // LANES)]
        up = [pltpu.roll(tile, 32, 1) for tile in tiles]
        down = [pltpu.roll(tile, LANES - 32, 1) for tile in tiles]
        zero = jnp.zeros((CZ, LANES), F32)
        out = []
        for i in range(CY // LANES):
            out.append(jnp.where(lane < 32, up[i - 1] if i else zero, up[i]))
            after = down[i + 1] if i + 1 < len(tiles) else zero
            out.append(jnp.where(lane < LANES - 32, down[i], after))
        return out

    def field_copy(delta):
        group = 4 + core - 2 * delta
        return pltpu.make_async_remote_copy(
            src_ref=fwin.at[t],
            dst_ref=fbuf.at[group],
            send_sem=f_send.at[delta + 2],
            recv_sem=f_recv.at[group],
            device_id=(t, 2 * (chip + delta)),
            device_id_type=MESH,
        )

    def chip_inside(delta):
        return (chip + delta >= 0) & (chip + delta < SPACE // 2)

    def field_sends(action):
        for delta in range(-2, 3):
            inside = chip_inside(delta)
            if delta == 0:
                inside = jnp.logical_not(even)

            @pl.when(inside)
            def _():
                action(field_copy(delta))

    def coarse_row(src, row):
        outside = (is_first & (row < 2)) | (is_last & (row >= 2 + CROWS))
        c, w, e = src[row], src[row - 1], src[row + 1]
        return update(
            c, w, e,
            shifted(c, 0, CZ, 1, czi), shifted(c, 0, CZ, -1, czi),
            shifted(c, 1, CY, 1, cyi), shifted(c, 1, CY, -1, cyi),
            dc[row], ac[row], mc[row], jnp.where(outside, 0.0, 0.3), 2.0,
        )

    def own_run():
        def first(row):
            rc1[row] = coarse_row(rc, row)

        def second(row):
            own[row - 2] = coarse_row(rc1, row)

        loop(1, 7, first)
        loop(2, 6, second)

    work_side(1 - far_side, True, lambda: None)

    def field_windows(row):
        for which, ref in enumerate((dc, ac, mc)):
            for j, value in enumerate(windows(ref[2 + row])):
                fwin[j, which, row] = value

    loop(0, CROWS, field_windows)

    @pl.when(even)
    def _():
        fbuf[4] = fwin[t]

    field_sends(lambda copy: copy.start())

    work_side(far_side, far_valid, own_run)

    def make_drift(row):
        now = restrict(u2[HALO + 2 * row] + u2[HALO + 2 * row + 1]) - own[row]
        now = now + jnp.where(t == 0, own[row], 0.0)
        for j, value in enumerate(windows(now)):
            win[j, row] = value

    loop(0, CROWS, make_drift)

    def win_copy(j, delta):
        group = 4 + core - 2 * delta
        return pltpu.make_async_remote_copy(
            src_ref=win.at[j],
            dst_ref=cbuf.at[t, group],
            send_sem=win_send.at[j, delta + 2],
            recv_sem=win_recv.at[t, group],
            device_id=(j, 2 * (chip + delta)),
            device_id_type=MESH,
        )

    halo_groups = (17 - 2 * t) // 4

    def win_sends(action):
        def run(j):
            for delta in (0, -1, 1, -2, 2):
                group = 4 + core - 2 * delta
                wanted = (group >= 4 - halo_groups) & (group <= 5 + halo_groups)
                wanted = wanted & chip_inside(delta) & (t < SLICES - 1)
                if delta == 0:
                    wanted = wanted & jnp.logical_not(even & (j == t))

                @pl.when(wanted)
                def _():
                    action(win_copy(j, delta))

        loop(0, SLICES, run)

    win_sends(lambda copy: copy.start())

    @pl.when(even & (t < SLICES - 1))
    def _():
        cbuf[t, 4] = win[t]

    fine_copy = pltpu.make_async_copy(u2.at[pl.ds(HALO, ROWS)], fine_out, out_sem)
    fine_copy.start()

    def result_copy(link, half):
        return pltpu.make_async_remote_copy(
            src_ref=gout.at[link, pl.ds(CROWS * half, CROWS)],
            dst_ref=gbuf.at[t],
            send_sem=g_send.at[link, half],
            recv_sem=g_recv.at[t],
            device_id=(link + 1, 2 * chip + half),
            device_id_type=MESH,
        )

    @pl.when(even)
    def _():
        zs = lax.broadcasted_iota(jnp.int32, (CROWS, CZ, LANES), 1)
        y = 64 * t - 32 + lax.broadcasted_iota(jnp.int32, (CROWS, CZ, LANES), 2)
        scale = jnp.where((y >= 0) & (y < CY), 0.3, 0.0)
        row_of = lax.broadcasted_iota(jnp.int32, (CROWS, CZ, LANES), 0) + (8 * chip - OWN)

        for group in range(GROUPS):
            source = 2 * chip - 4 + group

            @pl.when((source >= 0) & (source < SPACE))
            def _():
                if group != 4:
                    pltpu.make_async_remote_copy(
                        src_ref=fwin.at[0], dst_ref=fbuf.at[group], send_sem=f_send.at[0],
                        recv_sem=f_recv.at[group], device_id=(t, s + 1), device_id_type=MESH,
                    ).wait_recv()

            @pl.when((source < 0) | (source >= SPACE))
            def _():
                fbuf[group] = jnp.zeros((3, CROWS, CZ, LANES), F32)
                for tau in range(SLICES - 1):
                    cbuf[tau, group] = jnp.zeros((CROWS, CZ, LANES), F32)

        def wait_slice(tau):
            for group in range(4 - reach(tau), 6 + reach(tau)):
                source = 2 * chip - 4 + group
                expected = (source >= 0) & (source < SPACE)
                if group == 4:
                    expected = expected & (t != tau)

                @pl.when(expected)
                def _():
                    pltpu.make_async_remote_copy(
                        src_ref=win.at[0], dst_ref=cbuf.at[tau, group], send_sem=win_send.at[0, 0],
                        recv_sem=win_recv.at[tau, group], device_id=(t, s + 1), device_id_type=MESH,
                    ).wait_recv()

        def block(src, group):
            first = CROWS * group
            u = src[pl.ds(first + 3, CROWS + 2)]
            c, w, e = u[1 : 1 + CROWS], u[:CROWS], u[2:]
            row = row_of + first
            inside = (row >= 0) & (row < SPACE * CROWS)
            f = fbuf[group]
            return update(
                c, w, e,
                jnp.where(zs == 0, 0.0, pltpu.roll(c, 1, 1)),
                jnp.where(zs == CZ - 1, 0.0, pltpu.roll(c, CZ - 1, 1)),
                pltpu.roll(c, 1, 2), pltpu.roll(c, LANES - 1, 2),
                f[0], f[1], f[2], jnp.where(inside, scale, 0.0), 2.0,
            )

        def put(dst, group, value):
            dst[pl.ds(CROWS * group + 4, CROWS)] = value

        zero = jnp.zeros((CROWS, CZ, LANES), F32)
        for ref in (cw0, cw1):
            put(ref, -1, zero)
            put(ref, GROUPS, zero)

        def step_a(link):
            extent = (16 - 2 * link) // 4
            blocks(4 - extent, 6 + extent, lambda g: put(cw1, g, block(cw0, g)))

        def step_b(link):
            extent = reach(link + 1)

            def finish(g):
                value = block(cw1, g)
                if link < SLICES - 2:
                    put(cw0, g, value + cbuf[link + 1, g])
                return value

            for half in range(2):
                gout[link, CROWS * half : CROWS * (half + 1)] = finish(4 + half)

            @pl.when(t != link + 1)
            def _():
                result_copy(link, 0).start()

            @pl.when(t == link + 1)
            def _():
                gbuf[t] = gout[link, 0:CROWS]

            result_copy(link, 1).start()
            blocks(4 - extent, 4, finish)
            blocks(6, 6 + extent, finish)

        wait_slice(0)
        loop(0, GROUPS, lambda g: put(cw0, g, cbuf[0, g]))
        for link in range(SLICES - 1):
            step_a(link)
            if link < SLICES - 2:
                wait_slice(link + 1)
            step_b(link)

    @pl.when(t == 0)
    def _():
        diff_out[...] = own[...] - own[...]

    @pl.when(t > 0)
    def _():
        def wait_result(j):
            @pl.when(jnp.logical_not(even & (j == t)))
            def _():
                pltpu.make_async_remote_copy(
                    src_ref=gout.at[0, pl.ds(0, CROWS)], dst_ref=gbuf.at[j], send_sem=g_send.at[0, 0],
                    recv_sem=g_recv.at[j], device_id=(t, s + 1 - 2 * core), device_id_type=MESH,
                ).wait_recv()

        loop(0, SLICES, wait_result)

        def assemble(row):
            for i in range(CY // LANES):
                value = jnp.where(
                    lane < LANES // 2,
                    pltpu.roll(gbuf[2 * i, row], LANES - 32, 1),
                    pltpu.roll(gbuf[2 * i + 1, row], 32, 1),
                )
                where = slice(i * LANES, (i + 1) * LANES)
                diff_out[row, :, where] = value - own[row, :, where]

        loop(0, CROWS, assemble)

    fine_copy.wait()
    for index in range(len(PIECES)):
        halo_copy(index, 1 - far_to).wait_send()

    @pl.when(far_valid)
    def _():
        for index in range(len(PIECES)):
            halo_copy(index, far_to).wait_send()

    field_sends(lambda copy: copy.wait_send())
    win_sends(lambda copy: copy.wait_send())

    @pl.when(even)
    def _():
        for link in range(SLICES - 1):
            @pl.when(t != link + 1)
            def _():
                result_copy(link, 0).wait_send()

            result_copy(link, 1).wait_send()


def blocks(first, last, function):
    def run(i, carry):
        function(i)
        return carry

    lax.fori_loop(first, last, run, 0)


def correct_kernel(fine, diff, out):
    lane = lax.broadcasted_iota(jnp.int32, (CZ, LANES), 1)
    sub = lax.broadcasted_iota(jnp.int32, (CZ, LANES), 0)

    def run(row, carry):
        for tile in range(NY // LANES):
            index = lane // 2 + (LANES // 2) * (tile % 2)
            source = diff[row, :, (tile // 2) * LANES : (tile // 2 + 1) * LANES]
            value = jnp.take_along_axis(source, index, axis=1)
            where = slice(tile * LANES, (tile + 1) * LANES)
            for half in range(2):
                wide = jnp.take_along_axis(value, sub // 2 + 4 * half, axis=0)
                for x in range(2):
                    at = (2 * row + x, slice(8 * half, 8 * half + 8), where)
                    out[at] = fine[at] + wide
        return carry

    lax.fori_loop(0, CROWS, run, 0)


def body(start_states, dispersion, soil_class, sorption_k, sorption_n):
    vmem = pl.BlockSpec(memory_space=pltpu.VMEM)
    anywhere = pl.BlockSpec(memory_space=pl.ANY)
    smem = pl.BlockSpec(memory_space=pltpu.SMEM)
    dma = pltpu.SemaphoreType.DMA
    grid = (EXT, NZ, NY)
    coarse = (EXT // 2, CZ, CY)
    tile = (CZ, LANES)
    scratch = [pltpu.VMEM(grid, F32) for _ in range(4)]
    scratch += [pltpu.VMEM(grid, jnp.int32)]
    scratch += [pltpu.VMEM(grid, F32) for _ in range(2)]
    scratch += [pltpu.VMEM(coarse, F32) for _ in range(2)]
    scratch += [pltpu.VMEM((CROWS, CZ, CY), F32)]
    scratch += [pltpu.VMEM(coarse, F32) for _ in range(3)]
    scratch += [
        pltpu.VMEM((SLICES, CROWS) + tile, F32),
        pltpu.VMEM((SLICES, 3, CROWS) + tile, F32),
        pltpu.VMEM((SLICES - 1, GROUPS, CROWS) + tile, F32),
        pltpu.VMEM((GROUPS, 3, CROWS) + tile, F32),
        pltpu.VMEM((CHAIN_ROWS + 8,) + tile, F32),
        pltpu.VMEM((CHAIN_ROWS + 8,) + tile, F32),
        pltpu.VMEM((SLICES - 1, 2 * CROWS) + tile, F32),
        pltpu.VMEM((SLICES, CROWS) + tile, F32),
        dma((3,)),
        dma((len(PIECES), 2)),
        dma((len(PIECES), 2)),
        dma((SLICES, 5)),
        dma((SLICES - 1, GROUPS)),
        dma((5,)),
        dma((GROUPS,)),
        dma((SLICES - 1, 2)),
        dma((SLICES,)),
        dma,
    ]
    fine, diff = pl.pallas_call(
        main_kernel,
        out_shape=(
            jax.ShapeDtypeStruct((ROWS, NZ, NY), F32),
            jax.ShapeDtypeStruct((CROWS, CZ, CY), F32),
        ),
        in_specs=[smem, smem, anywhere, anywhere, anywhere],
        out_specs=(anywhere, vmem),
        scratch_shapes=scratch,
        compiler_params=pltpu.CompilerParams(
            collective_id=0, has_side_effects=True, vmem_limit_bytes=40 * 2**20
        ),
    )(sorption_k, sorption_n, start_states[0], dispersion, soil_class)
    out = pl.pallas_call(
        correct_kernel,
        out_shape=jax.ShapeDtypeStruct((ROWS, NZ, NY), F32),
        in_specs=[vmem, vmem],
        out_specs=vmem,
        compiler_params=pltpu.CompilerParams(vmem_limit_bytes=20 * 2**20),
    )(fine, diff)
    return out[None]


def solution(mesh):
    in_specs = (
        P("tm", "space", None, None),
        P("space", None, None),
        P("space", None, None),
        P(),
        P(),
    )
    out_specs = P("tm", "space", None, None)
    return jax.shard_map(body, mesh=mesh, in_specs=in_specs, out_specs=out_specs, check_vma=False)
```

```python
import functools

import jax
import jax.numpy as jnp
from jax import lax
from jax.experimental import pallas as pl
from jax.experimental.pallas import tpu as pltpu
from jax.sharding import PartitionSpec as P

MESH = pl.DeviceIdType.MESH
F32 = jnp.float32

SPEED_X = 0.3
SPEED_Z = 0.2
DENSITY = 2.0

ROWS = 8
HALO = 4
EXT = ROWS + 2 * HALO
NZ = 16
NY = 1024
CROWS = 4
CZ = 8
CY = 512
SLICES = 8
SPACE = 16
GROUPS = 10
CHAIN_ROWS = GROUPS * CROWS
OWN = 16
LANES = 128

PIECES = (
    (0, 2, 2, 12),
    (1, 3, 1, 12),
    (2, 3, 1, 12),
    (0, 0, 2, 14),
    (1, 2, 1, 13),
    (2, 2, 1, 13),
    (1, 1, 1, 14),
    (2, 1, 1, 14),
)

NEAR = ((0, 0, 1), (0, 0, -1), (1, 0, 0), (0, 1, 0), (0, -1, 0))
WIDE = ((0, 2, 0), (1, 1, 0), (1, -1, 0), (0, 0, 2), (0, 0, -2))
FAR = ((0, 0, 3), (0, 0, -3), (0, 2, 0), (0, 0, 4), (0, 0, -4))


def rows_of(group):
    return pl.ds(CROWS * group, CROWS)


def reach(tau):
    return (17 - 2 * tau) // 4


def shifted(c, axis, size, steps, index):
    rolled = pltpu.roll(c, steps % size, axis)
    return jnp.where(index == (0 if steps > 0 else size - 1), 0.0, rolled)


def update(c, w, e, zm, zp, ym, yp, d, a, m, scale, per_h):
    lap = ((w + e) + (zm + zp)) + ((ym + yp) - 6.0 * c)
    adv = (SPEED_X * per_h) * (c - w) + (SPEED_Z * per_h) * (c - zm)
    ret = 1.0 + a * jnp.exp(m * jnp.log(jnp.abs(c) + 0.1))
    return c + scale * ((d * lap - adv) / ret)


def main_kernel(
    k_in, n_in, start, disp, soil, fine_out, diff_out,
    k_ref, n_ref, u0, u1, u2, dx, cx, ax, mx, rc, rc1, own, dc, ac, mc, win, fwin,
    cbuf, fbuf, cw0, cw1, scales, gout, gbuf,
    local_sem, halo_send, halo_recv, win_send, win_recv, f_send, f_recv, g_send, g_recv, known,
):
    t = lax.axis_index("tm")
    s = lax.axis_index("space")
    chip = s // 2
    core = lax.rem(s, 2)
    even = core == 0
    is_first = s == 0
    is_last = s == SPACE - 1

    def clear(first):
        for ref in (u0, dx):
            ref[pl.ds(first, HALO)] = jnp.zeros((HALO, NZ, NY), F32)
        cx[pl.ds(first, HALO)] = jnp.zeros((HALO, NZ, NY), jnp.int32)

    def greet(semaphore, steps):
        for dx, dz, ds in steps:
            there = s + ds

            @pl.when((there >= 0) & (there < SPACE))
            def _():
                pl.semaphore_signal(
                    semaphore,
                    inc=1,
                    device_id=(2 * lax.rem(t // 2 + 4 + dz, 4) + lax.rem(t + dx, 2), there),
                    device_id_type=MESH,
                )

    def greeted(semaphore, steps):
        count = 0
        for _, _, ds in steps:
            count = count + ((s + ds >= 0) & (s + ds < SPACE)).astype(jnp.int32)
        pl.semaphore_wait(semaphore, count)

    barrier = pltpu.get_barrier_semaphore()
    greet(barrier, NEAR)

    local = [
        pltpu.make_async_copy(src, dst.at[pl.ds(HALO, ROWS)], local_sem.at[i])
        for i, (src, dst) in enumerate(((start, u0), (disp, dx), (soil, cx)))
    ]
    local += [
        pltpu.make_async_copy(k_in, k_ref, local_sem.at[3]),
        pltpu.make_async_copy(n_in, n_ref, local_sem.at[4]),
    ]
    for copy in local:
        copy.start()

    @pl.when(is_first)
    def _():
        clear(0)

    @pl.when(is_last)
    def _():
        clear(HALO + ROWS)

    greeted(barrier, NEAR)

    sources = (start, disp, soil)
    targets = (u0, dx, cx)

    def halo_copy(index, side):
        array, low, count, high = PIECES[index]
        first = jnp.where(side == 0, low, high)
        origin = jnp.where(side == 0, low + HALO, high - HALO - ROWS)
        return pltpu.make_async_remote_copy(
            src_ref=sources[array].at[pl.ds(origin, count)],
            dst_ref=targets[array].at[pl.ds(first, count)],
            send_sem=halo_send.at[index, side],
            recv_sem=halo_recv.at[index, side],
            device_id=(t, jnp.where(side == 0, s + 1, s - 1)),
            device_id_type=MESH,
        )

    far_to = 1 - core
    far_side = core
    far_valid = jnp.logical_not(is_first | is_last)

    @pl.when(far_valid)
    def _():
        for index in range(len(PIECES)):
            halo_copy(index, far_to).start()

    for index in range(len(PIECES)):
        halo_copy(index, 1 - far_to).start()

    greet(known.at[0], NEAR)

    for copy in local:
        copy.wait()

    lane = lax.broadcasted_iota(jnp.int32, (8, LANES), 1)
    k_table = jnp.zeros((8, LANES), F32)
    n_table = jnp.zeros((8, LANES), F32)
    for i in range(k_ref.shape[0]):
        k_table = jnp.where(lane == i, k_ref[i], k_table)
        n_table = jnp.where(lane == i, n_ref[i], n_table)
    compact = lax.rem(2 * lane, LANES)
    zi = lax.broadcasted_iota(jnp.int32, (NZ, NY), 0)
    yi = lax.broadcasted_iota(jnp.int32, (NZ, NY), 1)
    czi = lax.broadcasted_iota(jnp.int32, (CZ, CY), 0)
    cyi = lax.broadcasted_iota(jnp.int32, (CZ, CY), 1)

    def take(value, index):
        return jnp.take_along_axis(value, index, axis=1)

    def look_up(row):
        k_parts, m_parts = [], []
        for z in range(0, NZ, 8):
            k_line, m_line = [], []
            for y in range(0, NY, LANES):
                soil_now = cx[row, z : z + 8, y : y + LANES]
                k = take(k_table, soil_now)
                n = take(n_table, soil_now)
                m = n - 1.0
                ax[row, z : z + 8, y : y + LANES] = (DENSITY * k) * n
                mx[row, z : z + 8, y : y + LANES] = m
                k_line.append(k)
                m_line.append(m)
            k_parts.append(jnp.concatenate(k_line, axis=1))
            m_parts.append(jnp.concatenate(m_line, axis=1))
        return jnp.concatenate(k_parts, axis=0), jnp.concatenate(m_parts, axis=0)

    sub = lax.broadcasted_iota(jnp.int32, (8, LANES), 0)
    compact_z = lax.rem(2 * sub, 8)

    def restrict(total):
        out = []
        for i in range(CY // LANES):
            halves = []
            for half in range(2):
                y = (2 * i + half) * LANES
                parts = []
                for z in range(0, NZ, 8):
                    value = total[z : z + 8, y : y + LANES]
                    value = value + pltpu.roll(value, 7, 0)
                    parts.append(jnp.take_along_axis(value, compact_z, axis=0))
                value = jnp.where(sub < 4, parts[0], parts[1])
                value = value + pltpu.roll(value, LANES - 1, 1)
                halves.append(take(value, compact))
            out.append(jnp.where(lane < LANES // 2, halves[0], halves[1]))
        return 0.125 * jnp.concatenate(out, axis=1)

    def fields(p):
        k_low, m_low = look_up(2 * p)
        k_high, m_high = look_up(2 * p + 1)
        coarse_k = restrict(k_low + k_high)
        coarse_m = restrict(m_low + m_high)
        dc[p] = restrict(dx[2 * p] + dx[2 * p + 1])
        ac[p] = (DENSITY * coarse_k) * (coarse_m + 1.0)
        mc[p] = coarse_m

    def restrict_start(p):
        rc[p] = restrict(u0[2 * p] + u0[2 * p + 1])

    def fine_row(src, dst, row, shift=0):
        outside = (is_first & (row < HALO)) | (is_last & (row >= HALO + ROWS))
        c, w, e = src[row], src[row - 1], src[row + 1]
        dst[row - shift] = update(
            c, w, e,
            shifted(c, 0, NZ, 1, zi), shifted(c, 0, NZ, -1, zi),
            shifted(c, 1, NY, 1, yi), shifted(c, 1, NY, -1, yi),
            dx[row], ax[row], mx[row], jnp.where(outside, 0.0, 0.6), 1.0,
        )

    def loop(first, last, function):
        def run(i, carry):
            function(i)
            return carry

        lax.fori_loop(first, last, run, 0)

    loop(2, 6, fields)
    loop(2, 6, restrict_start)
    loop(5, 11, functools.partial(fine_row, u0, u1))
    loop(6, 10, functools.partial(fine_row, u1, u2))
    loop(7, 9, functools.partial(fine_row, u2, u1))
    greeted(known.at[0], NEAR)
    greet(known.at[1], WIDE)

    def diagonal(side, d):
        for k, (src, dst) in enumerate(((u0, u1), (u1, u2), (u2, u1), (u1, fine_out))):
            low = HALO - d + k
            fine_row(src, dst, jnp.where(side == 0, low, EXT - 1 - low), HALO if k == 3 else 0)

    def arrive(side, valid, *indices):
        @pl.when(valid)
        def _():
            for index in indices:
                halo_copy(index, side).wait_recv()

    def pair_of(side, p):
        return jnp.where(side == 0, p, EXT // 2 - 1 - p)

    def work_side(side, valid, early, between):
        arrive(side, valid, 0)
        diagonal(side, 0)
        restrict_start(pair_of(side, 1))
        arrive(side, valid, 1, 2)
        look_up(jnp.where(side == 0, 3, 12))
        diagonal(side, 1)
        early()
        arrive(side, valid, 3, 4, 5)
        fields(pair_of(side, 1))
        diagonal(side, 2)
        restrict_start(pair_of(side, 0))
        between()
        arrive(side, valid, 6, 7)
        look_up(jnp.where(side == 0, 1, 14))
        diagonal(side, 3)

    def windows(value):
        tiles = [value[:, i * LANES : (i + 1) * LANES] for i in range(CY // LANES)]
        up = [pltpu.roll(tile, 32, 1) for tile in tiles]
        down = [pltpu.roll(tile, LANES - 32, 1) for tile in tiles]
        zero = jnp.zeros((CZ, LANES), F32)
        out = []
        for i in range(CY // LANES):
            out.append(jnp.where(lane < 32, up[i - 1] if i else zero, up[i]))
            after = down[i + 1] if i + 1 < len(tiles) else zero
            out.append(jnp.where(lane < LANES - 32, down[i], after))
        return out

    def field_copy(delta):
        group = 4 + core - 2 * delta
        return pltpu.make_async_remote_copy(
            src_ref=fwin.at[t],
            dst_ref=fbuf.at[rows_of(group)],
            send_sem=f_send.at[delta + 2],
            recv_sem=f_recv.at[group],
            device_id=(t, 2 * (chip + delta)),
            device_id_type=MESH,
        )

    def chip_inside(delta):
        return (chip + delta >= 0) & (chip + delta < SPACE // 2)

    def field_sends(action):
        for delta in range(-2, 3):
            inside = chip_inside(delta)
            if delta == 0:
                inside = jnp.logical_not(even)

            @pl.when(inside)
            def _():
                action(field_copy(delta))

    def coarse_row(src, row):
        outside = (is_first & (row < 2)) | (is_last & (row >= 2 + CROWS))
        c, w, e = src[row], src[row - 1], src[row + 1]
        return update(
            c, w, e,
            shifted(c, 0, CZ, 1, czi), shifted(c, 0, CZ, -1, czi),
            shifted(c, 1, CY, 1, cyi), shifted(c, 1, CY, -1, cyi),
            dc[row], ac[row], mc[row], jnp.where(outside, 0.0, 0.3), 2.0,
        )

    def own_run():
        def first(row):
            rc1[row] = coarse_row(rc, row)

        def second(row):
            own[row - 2] = coarse_row(rc1, row)

        loop(1, 7, first)
        loop(2, 6, second)

    work_side(1 - far_side, True, lambda: None, lambda: None)

    def field_windows(row):
        for which, ref in enumerate((dc, ac, mc)):
            for j, value in enumerate(windows(ref[2 + row])):
                fwin[j, row, which] = value

    loop(0, CROWS, field_windows)

    @pl.when(even)
    def _():
        fbuf[OWN : OWN + CROWS] = fwin[t]

    greeted(known.at[1], WIDE)
    greet(known.at[2], FAR)

    def send_fields():
        @pl.when(far_valid)
        def _():
            for index in range(len(PIECES)):
                halo_copy(index, far_to).wait_send()

        greeted(known.at[2], FAR)
        field_sends(lambda copy: copy.start())

    work_side(far_side, far_valid, send_fields, own_run)

    def make_drift(row):
        now = restrict(fine_out[2 * row] + fine_out[2 * row + 1]) - own[row]
        now = now + jnp.where(t == 0, own[row], 0.0)
        for j, value in enumerate(windows(now)):
            win[j, row] = value

    loop(0, CROWS, make_drift)

    def win_copy(j, delta):
        group = 4 + core - 2 * delta
        return pltpu.make_async_remote_copy(
            src_ref=win.at[j],
            dst_ref=cbuf.at[t, rows_of(group)],
            send_sem=win_send.at[j, delta + 2],
            recv_sem=win_recv.at[t, group],
            device_id=(j, 2 * (chip + delta)),
            device_id_type=MESH,
        )

    halo_groups = (17 - 2 * t) // 4

    def win_sends(action):
        def run(j):
            for delta in (0, -1, 1, -2, 2):
                group = 4 + core - 2 * delta
                wanted = (group >= 4 - halo_groups) & (group <= 5 + halo_groups)
                wanted = wanted & chip_inside(delta) & (t < SLICES - 1)
                if delta == 0:
                    wanted = wanted & jnp.logical_not(even & (j == t))

                @pl.when(wanted)
                def _():
                    action(win_copy(j, delta))

        loop(0, SLICES, run)

    win_sends(lambda copy: copy.start())

    @pl.when(even & (t < SLICES - 1))
    def _():
        cbuf[t, OWN : OWN + CROWS] = win[t]

    def result_copy(link, half):
        return pltpu.make_async_remote_copy(
            src_ref=gout.at[link, pl.ds(CROWS * half, CROWS)],
            dst_ref=gbuf.at[t],
            send_sem=g_send.at[link, half],
            recv_sem=g_recv.at[t],
            device_id=(link + 1, 2 * chip + half),
            device_id_type=MESH,
        )

    @pl.when(even)
    def _():
        y = 64 * t - 32 + lane
        scale = jnp.where((y >= 0) & (y < CY), 0.3, 0.0)

        for group in range(GROUPS):
            source = 2 * chip - 4 + group

            @pl.when((source >= 0) & (source < SPACE))
            def _():
                if group != 4:
                    pltpu.make_async_remote_copy(
                        src_ref=fwin.at[0], dst_ref=fbuf.at[rows_of(group)], send_sem=f_send.at[0],
                        recv_sem=f_recv.at[group], device_id=(t, s + 1), device_id_type=MESH,
                    ).wait_recv()

            @pl.when((source < 0) | (source >= SPACE))
            def _():
                fbuf[rows_of(group)] = jnp.zeros((CROWS, 3, CZ, LANES), F32)
                for tau in range(SLICES - 1):
                    cbuf[tau, rows_of(group)] = jnp.zeros((CROWS, CZ, LANES), F32)

        def wait_slice(tau):
            for group in range(4 - reach(tau), 6 + reach(tau)):
                source = 2 * chip - 4 + group
                expected = (source >= 0) & (source < SPACE)
                if group == 4:
                    expected = expected & (t != tau)

                @pl.when(expected)
                def _():
                    pltpu.make_async_remote_copy(
                        src_ref=win.at[0], dst_ref=cbuf.at[tau, rows_of(group)], send_sem=win_send.at[0, 0],
                        recv_sem=win_recv.at[tau, group], device_id=(t, s + 1), device_id_type=MESH,
                    ).wait_recv()

        def block(src, dst, first, count, done=None):
            if count == 0:
                return
            c = src[pl.ds(first, count)]
            w = src[pl.ds(first - 1, count)]
            e = src[pl.ds(first + 1, count)]
            zs = lax.broadcasted_iota(jnp.int32, (count, CZ, LANES), 1)
            at = pl.ds(first, count)
            value = update(
                c, w, e,
                jnp.where(zs == 0, 0.0, pltpu.roll(c, 1, 1)),
                jnp.where(zs == CZ - 1, 0.0, pltpu.roll(c, CZ - 1, 1)),
                pltpu.roll(c, 1, 2), pltpu.roll(c, LANES - 1, 2),
                fbuf[at, 0], fbuf[at, 1], fbuf[at, 2], scales[at], 2.0,
            )
            if done is None:
                dst[at] = value
            else:
                done(at, value)

        def set_scale(row, carry):
            x = row + 8 * chip - OWN
            scales[row] = jnp.where((x >= 0) & (x < SPACE * CROWS), scale, 0.0)
            return carry

        lax.fori_loop(0, CHAIN_ROWS, set_scale, 0)

        wait_slice(0)
        for link in range(SLICES - 1):
            low = OWN - (SLICES - 1 - link) * 2 + 1
            own_last = OWN + 2 * CROWS
            source = cbuf.at[0] if link == 0 else cw0
            block(source, cw1, OWN, 2 * CROWS)
            block(source, cw1, low, OWN - low)
            block(source, cw1, own_last, OWN - low)
            low = low + 1
            if link < SLICES - 2:
                wait_slice(link + 1)

            def finish(at, value):
                if link < SLICES - 2:
                    cw0[at] = value + cbuf[link + 1, at]

            def finish_own(at, value):
                gout[link] = value
                finish(at, value)

            block(cw1, cw0, OWN, 2 * CROWS, finish_own)

            @pl.when(t != link + 1)
            def _():
                result_copy(link, 0).start()

            @pl.when(t == link + 1)
            def _():
                gbuf[t] = gout[link, 0:CROWS]

            result_copy(link, 1).start()
            block(cw1, cw0, low, OWN - low, finish)
            block(cw1, cw0, own_last, OWN - low, finish)

    @pl.when(t == 0)
    def _():
        diff_out[...] = own[...] - own[...]

    @pl.when(t > 0)
    def _():
        def wait_result(j):
            @pl.when(jnp.logical_not(even & (j == t)))
            def _():
                pltpu.make_async_remote_copy(
                    src_ref=gout.at[0, pl.ds(0, CROWS)], dst_ref=gbuf.at[j], send_sem=g_send.at[0, 0],
                    recv_sem=g_recv.at[j], device_id=(t, s + 1 - 2 * core), device_id_type=MESH,
                ).wait_recv()

        loop(0, SLICES, wait_result)

        def assemble(row):
            for i in range(CY // LANES):
                value = jnp.where(
                    lane < LANES // 2,
                    pltpu.roll(gbuf[2 * i, row], LANES - 32, 1),
                    pltpu.roll(gbuf[2 * i + 1, row], 32, 1),
                )
                where = slice(i * LANES, (i + 1) * LANES)
                diff_out[row, :, where] = value - own[row, :, where]

        loop(0, CROWS, assemble)

    for index in range(len(PIECES)):
        halo_copy(index, 1 - far_to).wait_send()

    field_sends(lambda copy: copy.wait_send())
    win_sends(lambda copy: copy.wait_send())

    @pl.when(even)
    def _():
        for link in range(SLICES - 1):
            @pl.when(t != link + 1)
            def _():
                result_copy(link, 0).wait_send()

            result_copy(link, 1).wait_send()


def correct_kernel(fine, diff, out):
    lane = lax.broadcasted_iota(jnp.int32, (CZ, LANES), 1)
    sub = lax.broadcasted_iota(jnp.int32, (CZ, LANES), 0)

    def run(row, carry):
        for tile in range(NY // LANES):
            index = lane // 2 + (LANES // 2) * (tile % 2)
            source = diff[row, :, (tile // 2) * LANES : (tile // 2 + 1) * LANES]
            value = jnp.take_along_axis(source, index, axis=1)
            where = slice(tile * LANES, (tile + 1) * LANES)
            for half in range(2):
                wide = jnp.take_along_axis(value, sub // 2 + 4 * half, axis=0)
                for x in range(2):
                    at = (2 * row + x, slice(8 * half, 8 * half + 8), where)
                    out[at] = fine[at] + wide
        return carry

    lax.fori_loop(0, CROWS, run, 0)


def body(start_states, dispersion, soil_class, sorption_k, sorption_n):
    vmem = pl.BlockSpec(memory_space=pltpu.VMEM)
    hbm = pl.BlockSpec(memory_space=pltpu.HBM)
    dma = pltpu.SemaphoreType.DMA
    grid = (EXT, NZ, NY)
    coarse = (EXT // 2, CZ, CY)
    tile = (CZ, LANES)
    scratch = [pltpu.SMEM((12,), F32) for _ in range(2)]
    scratch += [pltpu.VMEM(grid, F32) for _ in range(4)]
    scratch += [pltpu.VMEM(grid, jnp.int32)]
    scratch += [pltpu.VMEM(grid, F32) for _ in range(2)]
    scratch += [pltpu.VMEM(coarse, F32) for _ in range(2)]
    scratch += [pltpu.VMEM((CROWS, CZ, CY), F32)]
    scratch += [pltpu.VMEM(coarse, F32) for _ in range(3)]
    scratch += [
        pltpu.VMEM((SLICES, CROWS) + tile, F32),
        pltpu.VMEM((SLICES, CROWS, 3) + tile, F32),
        pltpu.VMEM((SLICES - 1, CHAIN_ROWS) + tile, F32),
        pltpu.VMEM((CHAIN_ROWS, 3) + tile, F32),
        pltpu.VMEM((CHAIN_ROWS,) + tile, F32),
        pltpu.VMEM((CHAIN_ROWS,) + tile, F32),
        pltpu.VMEM((CHAIN_ROWS,) + tile, F32),
        pltpu.VMEM((SLICES - 1, 2 * CROWS) + tile, F32),
        pltpu.VMEM((SLICES, CROWS) + tile, F32),
        dma((5,)),
        dma((len(PIECES), 2)),
        dma((len(PIECES), 2)),
        dma((SLICES, 5)),
        dma((SLICES - 1, GROUPS)),
        dma((5,)),
        dma((GROUPS,)),
        dma((SLICES - 1, 2)),
        dma((SLICES,)),
        pltpu.SemaphoreType.REGULAR((3,)),
    ]
    fine, diff = pl.pallas_call(
        main_kernel,
        out_shape=(
            pltpu.VMEM((ROWS, NZ, NY), F32),
            pltpu.VMEM((CROWS, CZ, CY), F32),
        ),
        in_specs=[hbm] * 5,
        out_specs=(vmem, vmem),
        scratch_shapes=scratch,
        compiler_params=pltpu.CompilerParams(
            collective_id=0, has_side_effects=True, vmem_limit_bytes=60 * 2**20
        ),
    )(sorption_k, sorption_n, start_states[0], dispersion, soil_class)
    out = pl.pallas_call(
        correct_kernel,
        out_shape=jax.ShapeDtypeStruct((ROWS, NZ, NY), F32),
        in_specs=[vmem, vmem],
        out_specs=vmem,
        compiler_params=pltpu.CompilerParams(vmem_limit_bytes=20 * 2**20),
    )(fine, diff)
    return out[None]


def solution(mesh):
    in_specs = (
        P("tm", "space", None, None),
        P("space", None, None),
        P("space", None, None),
        P(),
        P(),
    )
    out_specs = P("tm", "space", None, None)
    return jax.shard_map(body, mesh=mesh, in_specs=in_specs, out_specs=out_specs, check_vma=False)
```

```python
import functools

import jax
import jax.numpy as jnp
from jax import lax
from jax.experimental import pallas as pl
from jax.experimental.pallas import tpu as pltpu
from jax.sharding import PartitionSpec as P

MESH = pl.DeviceIdType.MESH
F32 = jnp.float32

SPEED_X = 0.3
SPEED_Z = 0.2
DENSITY = 2.0

ROWS = 8
HALO = 4
EXT = ROWS + 2 * HALO
NZ = 16
NY = 1024
CROWS = 4
CZ = 8
CY = 512
SLICES = 8
SPACE = 16
HALF = SPACE // 2
GROUPS = HALF + 4
PACKED = GROUPS * CROWS // 2
OWN_PACKED = HALF * CROWS // 2
WINDOWS = 16
LANES = 128

PIECES = (
    (0, 2, 2, 12),
    (1, 3, 1, 12),
    (2, 3, 1, 12),
    (0, 0, 2, 14),
    (1, 2, 1, 13),
    (2, 2, 1, 13),
    (1, 1, 1, 14),
    (2, 1, 1, 14),
)

PLANES = SLICES // 2
PASSES = (1, 2, 4)


def reach(tau):
    return (17 - 2 * tau) // 4


def host_of(half, side):
    return HALF // 2 + (HALF // 2) * half + 2 * side


def shifted(c, axis, size, steps, index):
    rolled = pltpu.roll(c, steps % size, axis)
    return jnp.where(index == (0 if steps > 0 else size - 1), 0.0, rolled)


def update(c, w, e, zm, zp, ym, yp, d, a, m, scale, per_h):
    lap = ((w + e) + (zm + zp)) + ((ym + yp) - 6.0 * c)
    adv = (SPEED_X * per_h) * (c - w) + (SPEED_Z * per_h) * (c - zm)
    ret = 1.0 + a * jnp.exp(m * jnp.log(jnp.abs(c) + 0.1))
    return c + scale * ((d * lap - adv) / ret)


def main_kernel(
    k_in, n_in, start, disp, soil, fine_out, diff_out,
    k_ref, n_ref, u0, u1, u2, dx, cx, ax, mx, rc, rc1, own, dc, ac, mc, win, fwin,
    cbuf, fbuf, cw0, cw1, gout, gbuf,
    local_sem, halo_send, halo_recv, win_send, win_recv, f_send, f_recv, g_send, g_recv, known,
):
    t = lax.axis_index("tm")
    s = lax.axis_index("space")
    core = lax.rem(s, 2)
    half = s // HALF
    is_host = (core == 0) & (s >= host_of(0, 0)) & (s <= host_of(1, 1))
    my_side = lax.rem((s - host_of(0, 0) + SPACE) // 2, 2)
    my_window = t + SLICES * my_side
    is_first = s == 0
    is_last = s == SPACE - 1

    def clear(first):
        for ref in (u0, dx):
            ref[pl.ds(first, HALO)] = jnp.zeros((HALO, NZ, NY), F32)
        cx[pl.ds(first, HALO)] = jnp.zeros((HALO, NZ, NY), jnp.int32)

    plane = t // 2

    def greet(semaphore, distance, planes=0):
        def tell(tt, ss):
            pl.semaphore_signal(semaphore, inc=1, device_id=(tt, ss), device_id_type=MESH)

        @pl.when(s >= distance)
        def _():
            tell(t, s - distance)

        @pl.when(s < SPACE - distance)
        def _():
            tell(t, s + distance)

        if planes:
            tell(t + 1 - 2 * lax.rem(t, 2), s)
            for step in range(1, PLANES):
                there = plane + planes * step

                @pl.when((there >= 0) & (there < PLANES))
                def _():
                    tell(2 * there, s)
                    tell(2 * there + 1, s)

    def greeted(semaphore, distance, planes=0):
        count = (s >= distance).astype(jnp.int32) + (s < SPACE - distance).astype(jnp.int32)
        if planes:
            count = count + 1 + 2 * (plane if planes == 1 else PLANES - 1 - plane)
        pl.semaphore_wait(semaphore, count)

    barrier = pltpu.get_barrier_semaphore()
    greet(barrier, 1, 1)

    local = [
        pltpu.make_async_copy(src, dst.at[pl.ds(HALO, ROWS)], local_sem.at[i])
        for i, (src, dst) in enumerate(((start, u0), (disp, dx), (soil, cx)))
    ]
    local += [
        pltpu.make_async_copy(k_in, k_ref, local_sem.at[3]),
        pltpu.make_async_copy(n_in, n_ref, local_sem.at[4]),
    ]
    for copy in local:
        copy.start()

    @pl.when(is_first)
    def _():
        clear(0)

    @pl.when(is_last)
    def _():
        clear(HALO + ROWS)

    greeted(barrier, 1, 1)

    sources = (start, disp, soil)
    targets = (u0, dx, cx)

    def halo_copy(index, side):
        array, low, count, high = PIECES[index]
        first = jnp.where(side == 0, low, high)
        origin = jnp.where(side == 0, low + HALO, high - HALO - ROWS)
        return pltpu.make_async_remote_copy(
            src_ref=sources[array].at[pl.ds(origin, count)],
            dst_ref=targets[array].at[pl.ds(first, count)],
            send_sem=halo_send.at[index, side],
            recv_sem=halo_recv.at[index, side],
            device_id=(t, jnp.where(side == 0, s + 1, s - 1)),
            device_id_type=MESH,
        )

    far_to = 1 - core
    far_side = core
    far_valid = jnp.logical_not(is_first | is_last)

    @pl.when(far_valid)
    def _():
        for index in range(len(PIECES)):
            halo_copy(index, far_to).start()

    for index in range(len(PIECES)):
        halo_copy(index, 1 - far_to).start()

    greet(known.at[0], PASSES[0], -1)

    for copy in local:
        copy.wait()

    lane = lax.broadcasted_iota(jnp.int32, (8, LANES), 1)
    k_table = jnp.zeros((8, LANES), F32)
    n_table = jnp.zeros((8, LANES), F32)
    for i in range(k_ref.shape[0]):
        k_table = jnp.where(lane == i, k_ref[i], k_table)
        n_table = jnp.where(lane == i, n_ref[i], n_table)
    compact = lax.rem(2 * lane, LANES)
    zi = lax.broadcasted_iota(jnp.int32, (NZ, NY), 0)
    yi = lax.broadcasted_iota(jnp.int32, (NZ, NY), 1)
    czi = lax.broadcasted_iota(jnp.int32, (CZ, CY), 0)
    cyi = lax.broadcasted_iota(jnp.int32, (CZ, CY), 1)

    def take(value, index):
        return jnp.take_along_axis(value, index, axis=1)

    def look_up(row):
        k_parts, m_parts = [], []
        for z in range(0, NZ, 8):
            k_line, m_line = [], []
            for y in range(0, NY, LANES):
                soil_now = cx[row, z : z + 8, y : y + LANES]
                k = take(k_table, soil_now)
                n = take(n_table, soil_now)
                m = n - 1.0
                ax[row, z : z + 8, y : y + LANES] = (DENSITY * k) * n
                mx[row, z : z + 8, y : y + LANES] = m
                k_line.append(k)
                m_line.append(m)
            k_parts.append(jnp.concatenate(k_line, axis=1))
            m_parts.append(jnp.concatenate(m_line, axis=1))
        return jnp.concatenate(k_parts, axis=0), jnp.concatenate(m_parts, axis=0)

    sub = lax.broadcasted_iota(jnp.int32, (8, LANES), 0)
    compact_z = lax.rem(2 * sub, 8)

    def restrict(total):
        out = []
        for i in range(CY // LANES):
            halves = []
            for half in range(2):
                y = (2 * i + half) * LANES
                parts = []
                for z in range(0, NZ, 8):
                    value = total[z : z + 8, y : y + LANES]
                    value = value + pltpu.roll(value, 7, 0)
                    parts.append(jnp.take_along_axis(value, compact_z, axis=0))
                value = jnp.where(sub < 4, parts[0], parts[1])
                value = value + pltpu.roll(value, LANES - 1, 1)
                halves.append(take(value, compact))
            out.append(jnp.where(lane < LANES // 2, halves[0], halves[1]))
        return 0.125 * jnp.concatenate(out, axis=1)

    def fields(p):
        k_low, m_low = look_up(2 * p)
        k_high, m_high = look_up(2 * p + 1)
        coarse_k = restrict(k_low + k_high)
        coarse_m = restrict(m_low + m_high)
        dc[p] = restrict(dx[2 * p] + dx[2 * p + 1])
        ac[p] = (DENSITY * coarse_k) * (coarse_m + 1.0)
        mc[p] = coarse_m

    def restrict_start(p):
        rc[p] = restrict(u0[2 * p] + u0[2 * p + 1])

    def fine_row(src, dst, row, shift=0):
        outside = (is_first & (row < HALO)) | (is_last & (row >= HALO + ROWS))
        c, w, e = src[row], src[row - 1], src[row + 1]
        dst[row - shift] = update(
            c, w, e,
            shifted(c, 0, NZ, 1, zi), shifted(c, 0, NZ, -1, zi),
            shifted(c, 1, NY, 1, yi), shifted(c, 1, NY, -1, yi),
            dx[row], ax[row], mx[row], jnp.where(outside, 0.0, 0.6), 1.0,
        )

    def loop(first, last, function):
        def run(i, carry):
            function(i)
            return carry

        lax.fori_loop(first, last, run, 0)

    loop(2, 6, fields)
    loop(2, 6, restrict_start)
    loop(5, 11, functools.partial(fine_row, u0, u1))
    loop(6, 10, functools.partial(fine_row, u1, u2))
    loop(7, 9, functools.partial(fine_row, u2, u1))
    greeted(known.at[0], PASSES[0], -1)
    greet(known.at[1], PASSES[1])

    def diagonal(side, d):
        for k, (src, dst) in enumerate(((u0, u1), (u1, u2), (u2, u1), (u1, fine_out))):
            low = HALO - d + k
            fine_row(src, dst, jnp.where(side == 0, low, EXT - 1 - low), HALO if k == 3 else 0)

    def arrive(side, valid, *indices):
        @pl.when(valid)
        def _():
            for index in indices:
                halo_copy(index, side).wait_recv()

    def pair_of(side, p):
        return jnp.where(side == 0, p, EXT // 2 - 1 - p)

    def work_side(side, valid, early, between):
        arrive(side, valid, 0)
        diagonal(side, 0)
        restrict_start(pair_of(side, 1))
        arrive(side, valid, 1, 2)
        look_up(jnp.where(side == 0, 3, 12))
        diagonal(side, 1)
        early()
        arrive(side, valid, 3, 4, 5)
        fields(pair_of(side, 1))
        diagonal(side, 2)
        restrict_start(pair_of(side, 0))
        between()
        arrive(side, valid, 6, 7)
        look_up(jnp.where(side == 0, 1, 14))
        diagonal(side, 3)

    def windows(first, second):
        def tiles(value):
            return [value[:, i * LANES : (i + 1) * LANES] for i in range(CY // LANES)]

        def roll(values, steps):
            return [pltpu.roll(value, steps % LANES, 1) for value in values]

        zero = jnp.zeros((CZ, LANES), F32)
        left = [roll(tiles(first), 16 - 32 * k) for k in range(4)]
        right = [roll(tiles(second), 80 - 32 * k) for k in range(4)]
        out = []
        for i in range(CY // LANES):
            for k in range(4):
                a, b = left[k][i], right[k][i]
                if k == 0:
                    a = jnp.where(lane < 16, left[k][i - 1] if i else zero, a)
                    b = jnp.where(lane < 80, right[k][i - 1] if i else zero, b)
                if k == 3:
                    last = i + 1 == CY // LANES
                    a = jnp.where(lane < 48, a, zero if last else left[k][i + 1])
                    b = jnp.where(lane < 112, b, zero if last else right[k][i + 1])
                out.append(jnp.where(lane < 64, a, b))
        return out

    def slot(source, to_half):
        return pl.ds(1 + 2 * (source - (HALF // 2) * to_half), 2)

    def to_half(other):
        return 1 - half if other else half

    def in_halo(groups):
        return jnp.where(half == 0, s >= HALF - groups, s < HALF + groups)

    def field_copy(side, other):
        return pltpu.make_async_remote_copy(
            src_ref=fwin.at[t + SLICES * side],
            dst_ref=fbuf.at[slot(s, to_half(other))],
            send_sem=f_send.at[side, other],
            recv_sem=f_recv.at[s],
            device_id=(t, host_of(to_half(other), side)),
            device_id_type=MESH,
        )

    def field_sends(action):
        for other in range(2):
            for side in range(2):
                if other:
                    wanted = in_halo(reach(0))
                else:
                    wanted = jnp.logical_not(is_host & (side == my_side))

                @pl.when(wanted)
                def _():
                    action(field_copy(side, other))

    def coarse_row(src, row):
        outside = (is_first & (row < 2)) | (is_last & (row >= 2 + CROWS))
        c, w, e = src[row], src[row - 1], src[row + 1]
        return update(
            c, w, e,
            shifted(c, 0, CZ, 1, czi), shifted(c, 0, CZ, -1, czi),
            shifted(c, 1, CY, 1, cyi), shifted(c, 1, CY, -1, cyi),
            dc[row], ac[row], mc[row], jnp.where(outside, 0.0, 0.3), 2.0,
        )

    def own_run():
        def first(row):
            rc1[row] = coarse_row(rc, row)

        def second(row):
            own[row - 2] = coarse_row(rc1, row)

        loop(1, 7, first)
        loop(2, 6, second)

    work_side(1 - far_side, True, lambda: None, lambda: None)

    def field_windows(q):
        for which, ref in enumerate((dc, ac, mc)):
            for j, value in enumerate(windows(ref[2 + 2 * q], ref[3 + 2 * q])):
                fwin[j, q, which] = value

    loop(0, CROWS // 2, field_windows)

    @pl.when(is_host)
    def _():
        fbuf[slot(s, half)] = fwin[my_window]

    greeted(known.at[1], PASSES[1])
    greet(known.at[2], PASSES[2])

    def send_fields():
        @pl.when(far_valid)
        def _():
            for index in range(len(PIECES)):
                halo_copy(index, far_to).wait_send()

        greeted(known.at[2], PASSES[2])
        field_sends(lambda copy: copy.start())

    work_side(far_side, far_valid, send_fields, own_run)

    def make_drift(q):
        def drift(row):
            now = restrict(fine_out[2 * row] + fine_out[2 * row + 1]) - own[row]
            return now + jnp.where(t == 0, own[row], 0.0)

        for j, value in enumerate(windows(drift(2 * q), drift(2 * q + 1))):
            win[j, q] = value

    loop(0, CROWS // 2, make_drift)

    def win_copy(j, other):
        return pltpu.make_async_remote_copy(
            src_ref=win.at[j],
            dst_ref=cbuf.at[t, slot(s, to_half(other))],
            send_sem=win_send.at[j, other],
            recv_sem=win_recv.at[t, s],
            device_id=(lax.rem(j, SLICES), host_of(to_half(other), j // SLICES)),
            device_id_type=MESH,
        )

    def win_sends(action):
        def run(j):
            @pl.when((t < SLICES - 1) & jnp.logical_not(is_host & (j == my_window)))
            def _():
                action(win_copy(j, 0))

            @pl.when((t < SLICES - 1) & in_halo((17 - 2 * t) // 4))
            def _():
                action(win_copy(j, 1))

        loop(0, WINDOWS, run)

    win_sends(lambda copy: copy.start())

    @pl.when(is_host & (t < SLICES - 1))
    def _():
        cbuf[t, slot(s, half)] = win[my_window]

    def result_copy(link, r):
        return pltpu.make_async_remote_copy(
            src_ref=gout.at[link, r],
            dst_ref=gbuf.at[my_window],
            send_sem=g_send.at[link, r],
            recv_sem=g_recv.at[my_window],
            device_id=(link + 1, HALF * half + r),
            device_id_type=MESH,
        )

    def result_sends(link, action):
        def run(r):
            @pl.when((t != link + 1) | (HALF * half + r != s))
            def _():
                action(result_copy(link, r))

        loop(0, HALF, run)

    @pl.when(is_host)
    def _():
        y = 32 * my_window - 16 + lax.rem(lane, 64)
        scale = jnp.where((y >= 0) & (y < CY), 0.3, 0.0)
        edge = jnp.zeros((1, CZ, LANES), F32)
        for row in (0, PACKED + 1):
            cbuf[0, row : row + 1] = edge

        def clear_row(row):
            cw0[row] = edge[0]
            cw1[row] = edge[0]

        loop(0, PACKED + 2, clear_row)

        def source(k):
            return jnp.where(half == 0, k, SPACE - 1 - k)

        for k in range(GROUPS):
            @pl.when(source(k) != s)
            def _():
                pltpu.make_async_remote_copy(
                    src_ref=fwin.at[0], dst_ref=fbuf.at[slot(source(k), half)], send_sem=f_send.at[0, 0],
                    recv_sem=f_recv.at[source(k)], device_id=(t, s + 1), device_id_type=MESH,
                ).wait_recv()

        def wait_slice(tau):
            for k in range(HALF + reach(tau)):
                @pl.when((source(k) != s) | (t != tau))
                def _():
                    pltpu.make_async_remote_copy(
                        src_ref=win.at[0], dst_ref=cbuf.at[tau, slot(source(k), half)],
                        send_sem=win_send.at[0, 0], recv_sem=win_recv.at[tau, source(k)],
                        device_id=(t, s + 1), device_id_type=MESH,
                    ).wait_recv()

        def block(src, first, count):
            u = src[pl.ds(first - 1, count + 2)]
            c = u[1 : count + 1]
            crossed = pltpu.roll(u, LANES // 2, 2)
            is_left = lax.broadcasted_iota(jnp.int32, (count, CZ, LANES), 2) < LANES // 2
            zs = lax.broadcasted_iota(jnp.int32, (count, CZ, LANES), 1)
            at = pl.ds(first, count)
            return update(
                c,
                jnp.where(is_left, crossed[:count], crossed[1 : count + 1]),
                jnp.where(is_left, crossed[1 : count + 1], crossed[2:]),
                jnp.where(zs == 0, 0.0, pltpu.roll(c, 1, 1)),
                jnp.where(zs == CZ - 1, 0.0, pltpu.roll(c, CZ - 1, 1)),
                pltpu.roll(c, 1, 2), pltpu.roll(c, LANES - 1, 2),
                fbuf[at, 0], fbuf[at, 1], fbuf[at, 2], scale, 2.0,
            )

        def condense(value):
            pairs = value.reshape(HALF, 2, CZ, LANES)
            a, b = pairs[:, 0], pairs[:, 1]
            at = lax.broadcasted_iota(jnp.int32, (HALF, CZ, LANES), 2) // 32
            front = jnp.where(at == 0, pltpu.roll(a, LANES - 16, 2), pltpu.roll(a, LANES - 48, 2))
            back = jnp.where(at == 2, pltpu.roll(b, 48, 2), pltpu.roll(b, 16, 2))
            return jnp.where(at < 2, front, back)

        own_first = 1 + (PACKED - OWN_PACKED) * half

        wait_slice(0)
        for link in range(SLICES - 1):
            src = cbuf.at[0] if link == 0 else cw0
            halo = (15 - (2 * link + 1)) // 2
            first = jnp.where(half == 0, 1 + OWN_PACKED, 1 + PACKED - OWN_PACKED - halo)
            cw1[pl.ds(own_first, OWN_PACKED)] = block(src, own_first, OWN_PACKED)
            if halo:
                cw1[pl.ds(first, halo)] = block(src, first, halo)
            last = link == SLICES - 2
            if not last:
                wait_slice(link + 1)
            value = block(cw1, own_first, OWN_PACKED)
            gout[link] = condense(value)
            result_sends(link, lambda copy: copy.start())

            @pl.when(t == link + 1)
            def _():
                gbuf[my_window] = gout[link, s - HALF * half]

            if not last:
                at = pl.ds(own_first, OWN_PACKED)
                cw0[at] = value + cbuf[link + 1, at]
            halo = (15 - (2 * link + 2)) // 2
            first = jnp.where(half == 0, 1 + OWN_PACKED, 1 + PACKED - OWN_PACKED - halo)
            if halo:
                at = pl.ds(first, halo)
                cw0[at] = block(cw1, first, halo) + cbuf[link + 1, at]

    @pl.when(t == 0)
    def _():
        diff_out[...] = own[...] - own[...]

    @pl.when(t > 0)
    def _():
        def wait_result(j):
            @pl.when(jnp.logical_not(is_host & (j == my_window)))
            def _():
                pltpu.make_async_remote_copy(
                    src_ref=gout.at[0, 0], dst_ref=gbuf.at[j], send_sem=g_send.at[0, 0],
                    recv_sem=g_recv.at[j], device_id=(t, s + 1 - 2 * core), device_id_type=MESH,
                ).wait_recv()

        loop(0, WINDOWS, wait_result)
        quarter = lane // 32

        def assemble(row):
            for i in range(CY // LANES):
                value = jnp.zeros((CZ, LANES), F32)
                for k in range(4):
                    steps = 32 * (k - row) % LANES
                    value = jnp.where(quarter == k, pltpu.roll(gbuf[4 * i + k], steps, 1), value)
                where = slice(i * LANES, (i + 1) * LANES)
                diff_out[row, :, where] = value - own[row, :, where]

        for row in range(CROWS):
            assemble(row)

    for index in range(len(PIECES)):
        halo_copy(index, 1 - far_to).wait_send()

    field_sends(lambda copy: copy.wait_send())
    win_sends(lambda copy: copy.wait_send())

    @pl.when(is_host)
    def _():
        for link in range(SLICES - 1):
            result_sends(link, lambda copy: copy.wait_send())


def correct_kernel(fine, diff, out):
    lane = lax.broadcasted_iota(jnp.int32, (CZ, LANES), 1)
    sub = lax.broadcasted_iota(jnp.int32, (CZ, LANES), 0)

    def run(row, carry):
        for tile in range(NY // LANES):
            index = lane // 2 + (LANES // 2) * (tile % 2)
            source = diff[row, :, (tile // 2) * LANES : (tile // 2 + 1) * LANES]
            value = jnp.take_along_axis(source, index, axis=1)
            where = slice(tile * LANES, (tile + 1) * LANES)
            for half in range(2):
                wide = jnp.take_along_axis(value, sub // 2 + 4 * half, axis=0)
                for x in range(2):
                    at = (2 * row + x, slice(8 * half, 8 * half + 8), where)
                    out[at] = fine[at] + wide
        return carry

    lax.fori_loop(0, CROWS, run, 0)


def body(start_states, dispersion, soil_class, sorption_k, sorption_n):
    vmem = pl.BlockSpec(memory_space=pltpu.VMEM)
    hbm = pl.BlockSpec(memory_space=pltpu.HBM)
    dma = pltpu.SemaphoreType.DMA
    grid = (EXT, NZ, NY)
    coarse = (EXT // 2, CZ, CY)
    tile = (CZ, LANES)
    scratch = [pltpu.SMEM((12,), F32) for _ in range(2)]
    scratch += [pltpu.VMEM(grid, F32) for _ in range(4)]
    scratch += [pltpu.VMEM(grid, jnp.int32)]
    scratch += [pltpu.VMEM(grid, F32) for _ in range(2)]
    scratch += [pltpu.VMEM(coarse, F32) for _ in range(2)]
    scratch += [pltpu.VMEM((CROWS, CZ, CY), F32)]
    scratch += [pltpu.VMEM(coarse, F32) for _ in range(3)]
    scratch += [
        pltpu.VMEM((WINDOWS, CROWS // 2) + tile, F32),
        pltpu.VMEM((WINDOWS, CROWS // 2, 3) + tile, F32),
        pltpu.VMEM((SLICES - 1, PACKED + 2) + tile, F32),
        pltpu.VMEM((PACKED + 2, 3) + tile, F32),
        pltpu.VMEM((PACKED + 2,) + tile, F32),
        pltpu.VMEM((PACKED + 2,) + tile, F32),
        pltpu.VMEM((SLICES - 1, HALF) + tile, F32),
        pltpu.VMEM((WINDOWS,) + tile, F32),
        dma((5,)),
        dma((len(PIECES), 2)),
        dma((len(PIECES), 2)),
        dma((WINDOWS, 2)),
        dma((SLICES - 1, SPACE)),
        dma((2, 2)),
        dma((SPACE,)),
        dma((SLICES - 1, HALF)),
        dma((WINDOWS,)),
        pltpu.SemaphoreType.REGULAR((3,)),
    ]
    fine, diff = pl.pallas_call(
        main_kernel,
        out_shape=(
            pltpu.VMEM((ROWS, NZ, NY), F32),
            pltpu.VMEM((CROWS, CZ, CY), F32),
        ),
        in_specs=[hbm] * 5,
        out_specs=(vmem, vmem),
        scratch_shapes=scratch,
        compiler_params=pltpu.CompilerParams(
            collective_id=0, has_side_effects=True, vmem_limit_bytes=60 * 2**20
        ),
    )(sorption_k, sorption_n, start_states[0], dispersion, soil_class)
    out = pl.pallas_call(
        correct_kernel,
        out_shape=jax.ShapeDtypeStruct((ROWS, NZ, NY), F32),
        in_specs=[vmem, vmem],
        out_specs=vmem,
        compiler_params=pltpu.CompilerParams(vmem_limit_bytes=20 * 2**20),
    )(fine, diff)
    return out[None]


def solution(mesh):
    in_specs = (
        P("tm", "space", None, None),
        P("space", None, None),
        P("space", None, None),
        P(),
        P(),
    )
    out_specs = P("tm", "space", None, None)
    return jax.shard_map(body, mesh=mesh, in_specs=in_specs, out_specs=out_specs, check_vma=False)
```

```python
import functools

import jax
import jax.numpy as jnp
from jax import lax
from jax.experimental import pallas as pl
from jax.experimental.pallas import tpu as pltpu
from jax.sharding import PartitionSpec as P

MESH = pl.DeviceIdType.MESH
F32 = jnp.float32

SPEED_X = 0.3
SPEED_Z = 0.2
DENSITY = 2.0

ROWS = 8
HALO = 4
EXT = ROWS + 2 * HALO
NZ = 16
NY = 1024
CROWS = 4
CZ = 8
CY = 512
SLICES = 8
SPACE = 16
HALF = SPACE // 2
GROUPS = HALF + 4
PACKED = GROUPS * CROWS // 2
OWN_PACKED = HALF * CROWS // 2
WINDOWS = 16
LANES = 128

PIECES = (
    (0, 2, 2, 12),
    (1, 3, 1, 12),
    (2, 3, 1, 12),
    (0, 0, 2, 14),
    (1, 2, 1, 13),
    (2, 2, 1, 13),
    (1, 1, 1, 14),
    (2, 1, 1, 14),
)

PLANES = SLICES // 2
PASSES = (1, 2, 4)


def reach(tau):
    return (17 - 2 * tau) // 4


def host_of(half, side):
    return HALF // 2 + (HALF // 2) * half + 2 * side


def shifted(c, axis, size, steps, index):
    rolled = pltpu.roll(c, steps % size, axis)
    return jnp.where(index == (0 if steps > 0 else size - 1), 0.0, rolled)


def update(c, w, e, zm, zp, ym, yp, d, a, m, scale, per_h):
    lap = ((w + e) + (zm + zp)) + ((ym + yp) - 6.0 * c)
    adv = (SPEED_X * per_h) * (c - w) + (SPEED_Z * per_h) * (c - zm)
    ret = 1.0 + a * jnp.exp(m * jnp.log(jnp.abs(c) + 0.1))
    return c + scale * ((d * lap - adv) / ret)


def main_kernel(
    k_in, n_in, start, disp, soil, fine_out, diff_out,
    k_ref, n_ref, u0, u1, u2, dx, cx, ax, mx, rc, rc1, own, dc, ac, mc, drift, win, fwin,
    cbuf, fbuf, cw0, cw1, gout, gbuf,
    local_sem, halo_send, halo_recv, win_send, win_recv, f_send, f_recv, g_send, g_recv, known,
):
    t = lax.axis_index("tm")
    s = lax.axis_index("space")
    core = lax.rem(s, 2)
    half = s // HALF
    is_host = (core == 0) & (s >= host_of(0, 0)) & (s <= host_of(1, 1))
    my_side = lax.rem((s - host_of(0, 0) + SPACE) // 2, 2)
    my_window = t + SLICES * my_side
    is_first = s == 0
    is_last = s == SPACE - 1

    def clear(first):
        for ref in (u0, dx):
            ref[pl.ds(first, HALO)] = jnp.zeros((HALO, NZ, NY), F32)
        cx[pl.ds(first, HALO)] = jnp.zeros((HALO, NZ, NY), jnp.int32)

    plane = t // 2

    def greet(semaphore, distance, planes=0):
        def tell(tt, ss):
            pl.semaphore_signal(semaphore, inc=1, device_id=(tt, ss), device_id_type=MESH)

        @pl.when(s >= distance)
        def _():
            tell(t, s - distance)

        @pl.when(s < SPACE - distance)
        def _():
            tell(t, s + distance)

        if planes:
            tell(t + 1 - 2 * lax.rem(t, 2), s)
            for step in range(1, PLANES):
                there = plane + planes * step

                @pl.when((there >= 0) & (there < PLANES))
                def _():
                    tell(2 * there, s)
                    tell(2 * there + 1, s)

    def greeted(semaphore, distance, planes=0):
        count = (s >= distance).astype(jnp.int32) + (s < SPACE - distance).astype(jnp.int32)
        if planes:
            count = count + 1 + 2 * (plane if planes == 1 else PLANES - 1 - plane)
        pl.semaphore_wait(semaphore, count)

    barrier = pltpu.get_barrier_semaphore()
    greet(barrier, 1, 1)

    local = [
        pltpu.make_async_copy(src, dst.at[pl.ds(HALO, ROWS)], local_sem.at[i])
        for i, (src, dst) in enumerate(((start, u0), (disp, dx), (soil, cx)))
    ]
    local += [
        pltpu.make_async_copy(k_in, k_ref, local_sem.at[3]),
        pltpu.make_async_copy(n_in, n_ref, local_sem.at[4]),
    ]
    for copy in local:
        copy.start()

    @pl.when(is_first)
    def _():
        clear(0)

    @pl.when(is_last)
    def _():
        clear(HALO + ROWS)

    greeted(barrier, 1, 1)

    sources = (start, disp, soil)
    targets = (u0, dx, cx)

    def halo_copy(index, side):
        array, low, count, high = PIECES[index]
        first = jnp.where(side == 0, low, high)
        origin = jnp.where(side == 0, low + HALO, high - HALO - ROWS)
        return pltpu.make_async_remote_copy(
            src_ref=sources[array].at[pl.ds(origin, count)],
            dst_ref=targets[array].at[pl.ds(first, count)],
            send_sem=halo_send.at[index, side],
            recv_sem=halo_recv.at[index, side],
            device_id=(t, jnp.where(side == 0, s + 1, s - 1)),
            device_id_type=MESH,
        )

    far_to = 1 - core
    far_side = core
    far_valid = jnp.logical_not(is_first | is_last)

    @pl.when(far_valid)
    def _():
        for index in range(len(PIECES)):
            halo_copy(index, far_to).start()

    for index in range(len(PIECES)):
        halo_copy(index, 1 - far_to).start()

    greet(known.at[0], PASSES[0], -1)

    for copy in local:
        copy.wait()

    lane = lax.broadcasted_iota(jnp.int32, (8, LANES), 1)
    k_table = jnp.zeros((8, LANES), F32)
    n_table = jnp.zeros((8, LANES), F32)
    for i in range(k_ref.shape[0]):
        k_table = jnp.where(lane == i, k_ref[i], k_table)
        n_table = jnp.where(lane == i, n_ref[i], n_table)
    compact = lax.rem(2 * lane, LANES)
    zi = lax.broadcasted_iota(jnp.int32, (NZ, NY), 0)
    yi = lax.broadcasted_iota(jnp.int32, (NZ, NY), 1)
    czi = lax.broadcasted_iota(jnp.int32, (CZ, CY), 0)
    cyi = lax.broadcasted_iota(jnp.int32, (CZ, CY), 1)

    def take(value, index):
        return jnp.take_along_axis(value, index, axis=1)

    def look_up(row):
        k_parts, m_parts = [], []
        for z in range(0, NZ, 8):
            k_line, m_line = [], []
            for y in range(0, NY, LANES):
                soil_now = cx[row, z : z + 8, y : y + LANES]
                k = take(k_table, soil_now)
                n = take(n_table, soil_now)
                m = n - 1.0
                ax[row, z : z + 8, y : y + LANES] = (DENSITY * k) * n
                mx[row, z : z + 8, y : y + LANES] = m
                k_line.append(k)
                m_line.append(m)
            k_parts.append(jnp.concatenate(k_line, axis=1))
            m_parts.append(jnp.concatenate(m_line, axis=1))
        return jnp.concatenate(k_parts, axis=0), jnp.concatenate(m_parts, axis=0)

    sub = lax.broadcasted_iota(jnp.int32, (8, LANES), 0)
    compact_z = lax.rem(2 * sub, 8)

    def restrict(total):
        out = []
        for i in range(CY // LANES):
            halves = []
            for half in range(2):
                y = (2 * i + half) * LANES
                parts = []
                for z in range(0, NZ, 8):
                    value = total[z : z + 8, y : y + LANES]
                    value = value + pltpu.roll(value, 7, 0)
                    parts.append(jnp.take_along_axis(value, compact_z, axis=0))
                value = jnp.where(sub < 4, parts[0], parts[1])
                value = value + pltpu.roll(value, LANES - 1, 1)
                halves.append(take(value, compact))
            out.append(jnp.where(lane < LANES // 2, halves[0], halves[1]))
        return 0.125 * jnp.concatenate(out, axis=1)

    def fields(p):
        k_low, m_low = look_up(2 * p)
        k_high, m_high = look_up(2 * p + 1)
        coarse_k = restrict(k_low + k_high)
        coarse_m = restrict(m_low + m_high)
        dc[p] = restrict(dx[2 * p] + dx[2 * p + 1])
        ac[p] = (DENSITY * coarse_k) * (coarse_m + 1.0)
        mc[p] = coarse_m

    def restrict_start(p):
        rc[p] = restrict(u0[2 * p] + u0[2 * p + 1])

    def fine_row(src, dst, row, shift=0):
        outside = (is_first & (row < HALO)) | (is_last & (row >= HALO + ROWS))
        c, w, e = src[row], src[row - 1], src[row + 1]
        dst[row - shift] = update(
            c, w, e,
            shifted(c, 0, NZ, 1, zi), shifted(c, 0, NZ, -1, zi),
            shifted(c, 1, NY, 1, yi), shifted(c, 1, NY, -1, yi),
            dx[row], ax[row], mx[row], jnp.where(outside, 0.0, 0.6), 1.0,
        )

    def loop(first, last, function):
        def run(i, carry):
            function(i)
            return carry

        lax.fori_loop(first, last, run, 0)

    loop(2, 6, fields)
    loop(2, 6, restrict_start)
    loop(5, 11, functools.partial(fine_row, u0, u1))
    loop(6, 10, functools.partial(fine_row, u1, u2))
    loop(7, 9, functools.partial(fine_row, u2, u1))
    greeted(known.at[0], PASSES[0], -1)
    greet(known.at[1], PASSES[1])

    def diagonal(side, d):
        for k, (src, dst) in enumerate(((u0, u1), (u1, u2), (u2, u1), (u1, fine_out))):
            low = HALO - d + k
            fine_row(src, dst, jnp.where(side == 0, low, EXT - 1 - low), HALO if k == 3 else 0)

    def arrive(side, valid, *indices):
        @pl.when(valid)
        def _():
            for index in indices:
                halo_copy(index, side).wait_recv()

    def pair_of(side, p):
        return jnp.where(side == 0, p, EXT // 2 - 1 - p)

    def work_side(side, valid, after=(None, None, None)):
        def then(index):
            if after[index] is not None:
                after[index]()

        arrive(side, valid, 0)
        diagonal(side, 0)
        restrict_start(pair_of(side, 1))
        then(0)
        arrive(side, valid, 1, 2)
        look_up(jnp.where(side == 0, 3, 12))
        diagonal(side, 1)
        then(1)
        arrive(side, valid, 3, 4, 5)
        fields(pair_of(side, 1))
        diagonal(side, 2)
        restrict_start(pair_of(side, 0))
        then(2)
        arrive(side, valid, 6, 7)
        look_up(jnp.where(side == 0, 1, 14))
        diagonal(side, 3)

    def windows(first, second):
        def tiles(value):
            return [value[:, i * LANES : (i + 1) * LANES] for i in range(CY // LANES)]

        def roll(values, steps):
            return [pltpu.roll(value, steps % LANES, 1) for value in values]

        zero = jnp.zeros((CZ, LANES), F32)
        left = [roll(tiles(first), 16 - 32 * k) for k in range(4)]
        right = [roll(tiles(second), 80 - 32 * k) for k in range(4)]
        out = []
        for i in range(CY // LANES):
            for k in range(4):
                a, b = left[k][i], right[k][i]
                if k == 0:
                    a = jnp.where(lane < 16, left[k][i - 1] if i else zero, a)
                    b = jnp.where(lane < 80, right[k][i - 1] if i else zero, b)
                if k == 3:
                    last = i + 1 == CY // LANES
                    a = jnp.where(lane < 48, a, zero if last else left[k][i + 1])
                    b = jnp.where(lane < 112, b, zero if last else right[k][i + 1])
                out.append(jnp.where(lane < 64, a, b))
        return out

    def slot(source, to_half):
        return pl.ds(1 + 2 * (source - (HALF // 2) * to_half), 2)

    def to_half(other):
        return 1 - half if other else half

    def in_halo(groups):
        return jnp.where(half == 0, s >= HALF - groups, s < HALF + groups)

    def field_copy(side, other):
        return pltpu.make_async_remote_copy(
            src_ref=fwin.at[t + SLICES * side],
            dst_ref=fbuf.at[slot(s, to_half(other))],
            send_sem=f_send.at[side, other],
            recv_sem=f_recv.at[s],
            device_id=(t, host_of(to_half(other), side)),
            device_id_type=MESH,
        )

    def field_sends(action):
        for other in range(2):
            for side in range(2):
                if other:
                    wanted = in_halo(reach(0))
                else:
                    wanted = jnp.logical_not(is_host & (side == my_side))

                @pl.when(wanted)
                def _():
                    action(field_copy(side, other))

    def coarse_row(src, row):
        outside = (is_first & (row < 2)) | (is_last & (row >= 2 + CROWS))
        c, w, e = src[row], src[row - 1], src[row + 1]
        return update(
            c, w, e,
            shifted(c, 0, CZ, 1, czi), shifted(c, 0, CZ, -1, czi),
            shifted(c, 1, CY, 1, cyi), shifted(c, 1, CY, -1, cyi),
            dc[row], ac[row], mc[row], jnp.where(outside, 0.0, 0.3), 2.0,
        )

    def from_far(row, rows):
        return jnp.where(far_side == 0, row, rows - 1 - row)

    def own_first(r):
        row = from_far(r, EXT // 2)
        rc1[row] = coarse_row(rc, row)

    def own_second(r):
        row = from_far(r, EXT // 2)
        own[row - 2] = coarse_row(rc1, row)

    def make_drift(r):
        row = from_far(r, CROWS)
        now = restrict(fine_out[2 * row] + fine_out[2 * row + 1]) - own[row]
        drift[row] = now + jnp.where(t == 0, own[row], 0.0)

    def drift_windows(r):
        q = from_far(r, CROWS // 2)
        for j, value in enumerate(windows(drift[2 * q], drift[2 * q + 1])):
            win[j, q] = value

    def own_early():
        loop(2, 7, own_first)
        loop(3, 6, own_second)

    def own_late():
        own_first(1)
        own_second(2)

    work_side(1 - far_side, True)

    def field_windows(q):
        for which, ref in enumerate((dc, ac, mc)):
            for j, value in enumerate(windows(ref[2 + 2 * q], ref[3 + 2 * q])):
                fwin[j, q, which] = value

    loop(0, CROWS // 2, field_windows)

    @pl.when(is_host)
    def _():
        fbuf[slot(s, half)] = fwin[my_window]

    greeted(known.at[1], PASSES[1])
    greet(known.at[2], PASSES[2])

    def send_fields():
        @pl.when(far_valid)
        def _():
            for index in range(len(PIECES)):
                halo_copy(index, far_to).wait_send()

        greeted(known.at[2], PASSES[2])
        field_sends(lambda copy: copy.start())
        loop(1, CROWS, make_drift)
        drift_windows(1)

    work_side(far_side, far_valid, (own_early, send_fields, own_late))
    make_drift(0)
    drift_windows(0)

    def win_copy(j, other):
        return pltpu.make_async_remote_copy(
            src_ref=win.at[j],
            dst_ref=cbuf.at[t, slot(s, to_half(other))],
            send_sem=win_send.at[j, other],
            recv_sem=win_recv.at[t, s],
            device_id=(lax.rem(j, SLICES), host_of(to_half(other), j // SLICES)),
            device_id_type=MESH,
        )

    def win_sends(action):
        def run(j):
            @pl.when((t < SLICES - 1) & jnp.logical_not(is_host & (j == my_window)))
            def _():
                action(win_copy(j, 0))

            @pl.when((t < SLICES - 1) & in_halo((17 - 2 * t) // 4))
            def _():
                action(win_copy(j, 1))

        loop(0, WINDOWS, run)

    win_sends(lambda copy: copy.start())

    @pl.when(is_host & (t < SLICES - 1))
    def _():
        cbuf[t, slot(s, half)] = win[my_window]

    def result_copy(link, r):
        return pltpu.make_async_remote_copy(
            src_ref=gout.at[link, r],
            dst_ref=gbuf.at[my_window],
            send_sem=g_send.at[link, r],
            recv_sem=g_recv.at[my_window],
            device_id=(link + 1, HALF * half + r),
            device_id_type=MESH,
        )

    def result_sends(link, action):
        def run(r):
            @pl.when((t != link + 1) | (HALF * half + r != s))
            def _():
                action(result_copy(link, r))

        loop(0, HALF, run)

    @pl.when(is_host)
    def _():
        y = 32 * my_window - 16 + lax.rem(lane, 64)
        scale = jnp.where((y >= 0) & (y < CY), 0.3, 0.0)
        edge = jnp.zeros((1, CZ, LANES), F32)
        for row in (0, PACKED + 1):
            cbuf[0, row : row + 1] = edge

        def clear_row(row):
            cw0[row] = edge[0]
            cw1[row] = edge[0]

        loop(0, PACKED + 2, clear_row)

        def source(k):
            return jnp.where(half == 0, k, SPACE - 1 - k)

        for k in range(GROUPS):
            @pl.when(source(k) != s)
            def _():
                pltpu.make_async_remote_copy(
                    src_ref=fwin.at[0], dst_ref=fbuf.at[slot(source(k), half)], send_sem=f_send.at[0, 0],
                    recv_sem=f_recv.at[source(k)], device_id=(t, s + 1), device_id_type=MESH,
                ).wait_recv()

        def wait_slice(tau):
            for k in range(HALF + reach(tau)):
                @pl.when((source(k) != s) | (t != tau))
                def _():
                    pltpu.make_async_remote_copy(
                        src_ref=win.at[0], dst_ref=cbuf.at[tau, slot(source(k), half)],
                        send_sem=win_send.at[0, 0], recv_sem=win_recv.at[tau, source(k)],
                        device_id=(t, s + 1), device_id_type=MESH,
                    ).wait_recv()

        def block(src, first, count):
            u = src[pl.ds(first - 1, count + 2)]
            c = u[1 : count + 1]
            crossed = pltpu.roll(u, LANES // 2, 2)
            is_left = lax.broadcasted_iota(jnp.int32, (count, CZ, LANES), 2) < LANES // 2
            zs = lax.broadcasted_iota(jnp.int32, (count, CZ, LANES), 1)
            at = pl.ds(first, count)
            return update(
                c,
                jnp.where(is_left, crossed[:count], crossed[1 : count + 1]),
                jnp.where(is_left, crossed[1 : count + 1], crossed[2:]),
                jnp.where(zs == 0, 0.0, pltpu.roll(c, 1, 1)),
                jnp.where(zs == CZ - 1, 0.0, pltpu.roll(c, CZ - 1, 1)),
                pltpu.roll(c, 1, 2), pltpu.roll(c, LANES - 1, 2),
                fbuf[at, 0], fbuf[at, 1], fbuf[at, 2], scale, 2.0,
            )

        def condense(value):
            pairs = value.reshape(HALF, 2, CZ, LANES)
            a, b = pairs[:, 0], pairs[:, 1]
            at = lax.broadcasted_iota(jnp.int32, (HALF, CZ, LANES), 2) // 32
            front = jnp.where(at == 0, pltpu.roll(a, LANES - 16, 2), pltpu.roll(a, LANES - 48, 2))
            back = jnp.where(at == 2, pltpu.roll(b, 48, 2), pltpu.roll(b, 16, 2))
            return jnp.where(at < 2, front, back)

        first_own = 1 + (PACKED - OWN_PACKED) * half

        wait_slice(0)
        for link in range(SLICES - 1):
            src = cbuf.at[0] if link == 0 else cw0
            halo = (15 - (2 * link + 1)) // 2
            first = jnp.where(half == 0, 1 + OWN_PACKED, 1 + PACKED - OWN_PACKED - halo)
            cw1[pl.ds(first_own, OWN_PACKED)] = block(src, first_own, OWN_PACKED)
            if halo:
                cw1[pl.ds(first, halo)] = block(src, first, halo)
            last = link == SLICES - 2
            if not last:
                wait_slice(link + 1)
            value = block(cw1, first_own, OWN_PACKED)
            gout[link] = condense(value)
            result_sends(link, lambda copy: copy.start())

            @pl.when(t == link + 1)
            def _():
                gbuf[my_window] = gout[link, s - HALF * half]

            if not last:
                at = pl.ds(first_own, OWN_PACKED)
                cw0[at] = value + cbuf[link + 1, at]
            halo = (15 - (2 * link + 2)) // 2
            first = jnp.where(half == 0, 1 + OWN_PACKED, 1 + PACKED - OWN_PACKED - halo)
            if halo:
                at = pl.ds(first, halo)
                cw0[at] = block(cw1, first, halo) + cbuf[link + 1, at]

    @pl.when(t == 0)
    def _():
        diff_out[...] = own[...] - own[...]

    @pl.when(t > 0)
    def _():
        def wait_result(j):
            @pl.when(jnp.logical_not(is_host & (j == my_window)))
            def _():
                pltpu.make_async_remote_copy(
                    src_ref=gout.at[0, 0], dst_ref=gbuf.at[j], send_sem=g_send.at[0, 0],
                    recv_sem=g_recv.at[j], device_id=(t, s + 1 - 2 * core), device_id_type=MESH,
                ).wait_recv()

        loop(0, WINDOWS, wait_result)
        quarter = lane // 32

        def assemble(row):
            for i in range(CY // LANES):
                value = jnp.zeros((CZ, LANES), F32)
                for k in range(4):
                    steps = 32 * (k - row) % LANES
                    value = jnp.where(quarter == k, pltpu.roll(gbuf[4 * i + k], steps, 1), value)
                where = slice(i * LANES, (i + 1) * LANES)
                diff_out[row, :, where] = value - own[row, :, where]

        for row in range(CROWS):
            assemble(row)

    for index in range(len(PIECES)):
        halo_copy(index, 1 - far_to).wait_send()

    field_sends(lambda copy: copy.wait_send())
    win_sends(lambda copy: copy.wait_send())

    @pl.when(is_host)
    def _():
        for link in range(SLICES - 1):
            result_sends(link, lambda copy: copy.wait_send())


def correct_kernel(fine, diff, out, result, sems):
    lane = lax.broadcasted_iota(jnp.int32, (CZ, LANES), 1)
    sub = lax.broadcasted_iota(jnp.int32, (CZ, LANES), 0)

    def copy(row):
        rows = pl.ds(2 * row, 2)
        return pltpu.make_async_copy(result.at[rows], out.at[rows], sems.at[row])

    for row in range(CROWS):
        for tile in range(NY // LANES):
            index = lane // 2 + (LANES // 2) * (tile % 2)
            source = diff[row, :, (tile // 2) * LANES : (tile // 2 + 1) * LANES]
            value = jnp.take_along_axis(source, index, axis=1)
            where = slice(tile * LANES, (tile + 1) * LANES)
            for half in range(2):
                wide = jnp.take_along_axis(value, sub // 2 + 4 * half, axis=0)
                for x in range(2):
                    at = (2 * row + x, slice(8 * half, 8 * half + 8), where)
                    result[at] = fine[at] + wide
        copy(row).start()
    for row in range(CROWS):
        copy(row).wait()


def body(start_states, dispersion, soil_class, sorption_k, sorption_n):
    vmem = pl.BlockSpec(memory_space=pltpu.VMEM)
    hbm = pl.BlockSpec(memory_space=pltpu.HBM)
    dma = pltpu.SemaphoreType.DMA
    grid = (EXT, NZ, NY)
    coarse = (EXT // 2, CZ, CY)
    tile = (CZ, LANES)
    scratch = [pltpu.SMEM((12,), F32) for _ in range(2)]
    scratch += [pltpu.VMEM(grid, F32) for _ in range(4)]
    scratch += [pltpu.VMEM(grid, jnp.int32)]
    scratch += [pltpu.VMEM(grid, F32) for _ in range(2)]
    scratch += [pltpu.VMEM(coarse, F32) for _ in range(2)]
    scratch += [pltpu.VMEM((CROWS, CZ, CY), F32)]
    scratch += [pltpu.VMEM(coarse, F32) for _ in range(3)]
    scratch += [pltpu.VMEM((CROWS, CZ, CY), F32)]
    scratch += [
        pltpu.VMEM((WINDOWS, CROWS // 2) + tile, F32),
        pltpu.VMEM((WINDOWS, CROWS // 2, 3) + tile, F32),
        pltpu.VMEM((SLICES - 1, PACKED + 2) + tile, F32),
        pltpu.VMEM((PACKED + 2, 3) + tile, F32),
        pltpu.VMEM((PACKED + 2,) + tile, F32),
        pltpu.VMEM((PACKED + 2,) + tile, F32),
        pltpu.VMEM((SLICES - 1, HALF) + tile, F32),
        pltpu.VMEM((WINDOWS,) + tile, F32),
        dma((5,)),
        dma((len(PIECES), 2)),
        dma((len(PIECES), 2)),
        dma((WINDOWS, 2)),
        dma((SLICES - 1, SPACE)),
        dma((2, 2)),
        dma((SPACE,)),
        dma((SLICES - 1, HALF)),
        dma((WINDOWS,)),
        pltpu.SemaphoreType.REGULAR((3,)),
    ]
    fine, diff = pl.pallas_call(
        main_kernel,
        out_shape=(
            pltpu.VMEM((ROWS, NZ, NY), F32),
            pltpu.VMEM((CROWS, CZ, CY), F32),
        ),
        in_specs=[hbm] * 5,
        out_specs=(vmem, vmem),
        scratch_shapes=scratch,
        compiler_params=pltpu.CompilerParams(
            collective_id=0, has_side_effects=True, vmem_limit_bytes=60 * 2**20
        ),
    )(sorption_k, sorption_n, start_states[0], dispersion, soil_class)
    out = pl.pallas_call(
        correct_kernel,
        out_shape=jax.ShapeDtypeStruct((ROWS, NZ, NY), F32),
        in_specs=[vmem, vmem],
        out_specs=hbm,
        scratch_shapes=[pltpu.VMEM((ROWS, NZ, NY), F32), dma((CROWS,))],
        compiler_params=pltpu.CompilerParams(vmem_limit_bytes=20 * 2**20),
    )(fine, diff)
    return out[None]


def solution(mesh):
    in_specs = (
        P("tm", "space", None, None),
        P("space", None, None),
        P("space", None, None),
        P(),
        P(),
    )
    out_specs = P("tm", "space", None, None)
    return jax.shard_map(body, mesh=mesh, in_specs=in_specs, out_specs=out_specs, check_vma=False)
```

```python
import functools

import jax
import jax.numpy as jnp
from jax import lax
from jax.experimental import pallas as pl
from jax.experimental.pallas import tpu as pltpu
from jax.sharding import PartitionSpec as P

MESH = pl.DeviceIdType.MESH
F32 = jnp.float32

SPEED_X = 0.3
SPEED_Z = 0.2
DENSITY = 2.0

ROWS = 8
HALO = 4
EXT = ROWS + 2 * HALO
NZ = 16
NY = 1024
CROWS = 4
CZ = 8
CY = 512
SLICES = 8
SPACE = 16
HALF = SPACE // 2
GROUPS = HALF + 4
PACKED = GROUPS * CROWS // 2
OWN_PACKED = HALF * CROWS // 2
WINDOWS = 16
LANES = 128

PIECES = (
    (0, 2, 2, 12),
    (1, 3, 1, 12),
    (2, 3, 1, 12),
    (0, 0, 2, 14),
    (1, 2, 1, 13),
    (2, 2, 1, 13),
    (1, 1, 1, 14),
    (2, 1, 1, 14),
)

PLANES = SLICES // 2
PASSES = (1, 2, 4)


def reach(tau):
    return (17 - 2 * tau) // 4


def host_of(half, side):
    return HALF // 2 + (HALF // 2) * half + 2 * side


def shifted(c, axis, size, steps, index):
    rolled = pltpu.roll(c, steps % size, axis)
    return jnp.where(index == (0 if steps > 0 else size - 1), 0.0, rolled)


def update(c, w, e, zm, zp, ym, yp, d, a, m, scale, per_h):
    lap = ((w + e) + (zm + zp)) + ((ym + yp) - 6.0 * c)
    adv = (SPEED_X * per_h) * (c - w) + (SPEED_Z * per_h) * (c - zm)
    ret = 1.0 + a * jnp.exp(m * jnp.log(jnp.abs(c) + 0.1))
    return c + scale * ((d * lap - adv) / ret)


def main_kernel(
    k_in, n_in, start, disp, soil, fine_out, diff_out,
    k_ref, n_ref, u0, u1, u2, dx, cx, ax, mx, rc, rc1, own, dc, ac, mc, drift, win, fwin,
    cbuf, fbuf, cw0, cw1, gout, gbuf,
    local_sem, halo_send, halo_recv, win_send, win_recv, f_send, f_recv, g_send, g_recv, known,
):
    t = lax.axis_index("tm")
    s = lax.axis_index("space")
    core = lax.rem(s, 2)
    half = s // HALF
    is_host = (core == 0) & (s >= host_of(0, 0)) & (s <= host_of(1, 1))
    my_side = lax.rem((s - host_of(0, 0) + SPACE) // 2, 2)
    my_window = t + SLICES * my_side
    is_first = s == 0
    is_last = s == SPACE - 1

    def clear(first):
        for ref in (u0, dx):
            ref[pl.ds(first, HALO)] = jnp.zeros((HALO, NZ, NY), F32)
        cx[pl.ds(first, HALO)] = jnp.zeros((HALO, NZ, NY), jnp.int32)

    plane = t // 2

    def greet(semaphore, distance, planes=0):
        def tell(tt, ss):
            pl.semaphore_signal(semaphore, inc=1, device_id=(tt, ss), device_id_type=MESH)

        @pl.when(s >= distance)
        def _():
            tell(t, s - distance)

        @pl.when(s < SPACE - distance)
        def _():
            tell(t, s + distance)

        if planes:
            tell(t + 1 - 2 * lax.rem(t, 2), s)
            for step in range(1, PLANES):
                there = plane + planes * step

                @pl.when((there >= 0) & (there < PLANES))
                def _():
                    tell(2 * there, s)
                    tell(2 * there + 1, s)

    def greeted(semaphore, distance, planes=0):
        count = (s >= distance).astype(jnp.int32) + (s < SPACE - distance).astype(jnp.int32)
        if planes:
            count = count + 1 + 2 * (plane if planes == 1 else PLANES - 1 - plane)
        pl.semaphore_wait(semaphore, count)

    barrier = pltpu.get_barrier_semaphore()
    greet(barrier, 1, 1)

    local = [
        pltpu.make_async_copy(src, dst.at[pl.ds(HALO, ROWS)], local_sem.at[i])
        for i, (src, dst) in enumerate(((start, u0), (disp, dx), (soil, cx)))
    ]
    local += [
        pltpu.make_async_copy(k_in, k_ref, local_sem.at[3]),
        pltpu.make_async_copy(n_in, n_ref, local_sem.at[4]),
    ]
    for copy in local:
        copy.start()

    @pl.when(is_first)
    def _():
        clear(0)

    @pl.when(is_last)
    def _():
        clear(HALO + ROWS)

    for copy in local:
        copy.wait()

    greeted(barrier, 1, 1)

    targets = (u0, dx, cx)

    def halo_copy(index, side):
        array, low, count, high = PIECES[index]
        first = jnp.where(side == 0, low, high)
        origin = jnp.where(side == 0, low + ROWS, high - ROWS)
        return pltpu.make_async_remote_copy(
            src_ref=targets[array].at[pl.ds(origin, count)],
            dst_ref=targets[array].at[pl.ds(first, count)],
            send_sem=halo_send.at[index, side],
            recv_sem=halo_recv.at[index, side],
            device_id=(t, jnp.where(side == 0, s + 1, s - 1)),
            device_id_type=MESH,
        )

    far_to = 1 - core
    far_side = core
    far_valid = jnp.logical_not(is_first | is_last)

    @pl.when(far_valid)
    def _():
        for index in range(len(PIECES)):
            halo_copy(index, far_to).start()

    for index in range(len(PIECES)):
        halo_copy(index, 1 - far_to).start()

    greet(known.at[0], PASSES[0], -1)

    lane = lax.broadcasted_iota(jnp.int32, (8, LANES), 1)
    k_table = jnp.zeros((8, LANES), F32)
    n_table = jnp.zeros((8, LANES), F32)
    for i in range(k_ref.shape[0]):
        k_table = jnp.where(lane == i, k_ref[i], k_table)
        n_table = jnp.where(lane == i, n_ref[i], n_table)
    compact = lax.rem(2 * lane, LANES)
    zi = lax.broadcasted_iota(jnp.int32, (NZ, NY), 0)
    yi = lax.broadcasted_iota(jnp.int32, (NZ, NY), 1)
    czi = lax.broadcasted_iota(jnp.int32, (CZ, CY), 0)
    cyi = lax.broadcasted_iota(jnp.int32, (CZ, CY), 1)

    def take(value, index):
        return jnp.take_along_axis(value, index, axis=1)

    def look_up(row):
        k_parts, m_parts = [], []
        for z in range(0, NZ, 8):
            k_line, m_line = [], []
            for y in range(0, NY, LANES):
                soil_now = cx[row, z : z + 8, y : y + LANES]
                k = take(k_table, soil_now)
                n = take(n_table, soil_now)
                m = n - 1.0
                ax[row, z : z + 8, y : y + LANES] = (DENSITY * k) * n
                mx[row, z : z + 8, y : y + LANES] = m
                k_line.append(k)
                m_line.append(m)
            k_parts.append(jnp.concatenate(k_line, axis=1))
            m_parts.append(jnp.concatenate(m_line, axis=1))
        return jnp.concatenate(k_parts, axis=0), jnp.concatenate(m_parts, axis=0)

    sub = lax.broadcasted_iota(jnp.int32, (8, LANES), 0)
    compact_z = lax.rem(2 * sub, 8)

    def restrict(total):
        out = []
        for i in range(CY // LANES):
            halves = []
            for half in range(2):
                y = (2 * i + half) * LANES
                parts = []
                for z in range(0, NZ, 8):
                    value = total[z : z + 8, y : y + LANES]
                    value = value + pltpu.roll(value, 7, 0)
                    parts.append(jnp.take_along_axis(value, compact_z, axis=0))
                value = jnp.where(sub < 4, parts[0], parts[1])
                value = value + pltpu.roll(value, LANES - 1, 1)
                halves.append(take(value, compact))
            out.append(jnp.where(lane < LANES // 2, halves[0], halves[1]))
        return 0.125 * jnp.concatenate(out, axis=1)

    def fields(p):
        k_low, m_low = look_up(2 * p)
        k_high, m_high = look_up(2 * p + 1)
        coarse_k = restrict(k_low + k_high)
        coarse_m = restrict(m_low + m_high)
        dc[p] = restrict(dx[2 * p] + dx[2 * p + 1])
        ac[p] = (DENSITY * coarse_k) * (coarse_m + 1.0)
        mc[p] = coarse_m

    def restrict_start(p):
        rc[p] = restrict(u0[2 * p] + u0[2 * p + 1])

    def fine_row(src, dst, row, shift=0):
        outside = (is_first & (row < HALO)) | (is_last & (row >= HALO + ROWS))
        c, w, e = src[row], src[row - 1], src[row + 1]
        dst[row - shift] = update(
            c, w, e,
            shifted(c, 0, NZ, 1, zi), shifted(c, 0, NZ, -1, zi),
            shifted(c, 1, NY, 1, yi), shifted(c, 1, NY, -1, yi),
            dx[row], ax[row], mx[row], jnp.where(outside, 0.0, 0.6), 1.0,
        )

    def loop(first, last, function):
        def run(i, carry):
            function(i)
            return carry

        lax.fori_loop(first, last, run, 0)

    loop(2, 6, fields)
    loop(2, 6, restrict_start)
    loop(5, 11, functools.partial(fine_row, u0, u1))
    loop(6, 10, functools.partial(fine_row, u1, u2))
    loop(7, 9, functools.partial(fine_row, u2, u1))
    greeted(known.at[0], PASSES[0], -1)
    greet(known.at[1], PASSES[1])

    def diagonal(side, d):
        for k, (src, dst) in enumerate(((u0, u1), (u1, u2), (u2, u1), (u1, fine_out))):
            low = HALO - d + k
            fine_row(src, dst, jnp.where(side == 0, low, EXT - 1 - low), HALO if k == 3 else 0)

    def arrive(side, valid, *indices):
        @pl.when(valid)
        def _():
            for index in indices:
                halo_copy(index, side).wait_recv()

    def pair_of(side, p):
        return jnp.where(side == 0, p, EXT // 2 - 1 - p)

    def work_side(side, valid, after=(None, None, None)):
        def then(index):
            if after[index] is not None:
                after[index]()

        arrive(side, valid, 0)
        diagonal(side, 0)
        restrict_start(pair_of(side, 1))
        then(0)
        arrive(side, valid, 1, 2)
        look_up(jnp.where(side == 0, 3, 12))
        diagonal(side, 1)
        then(1)
        arrive(side, valid, 3, 4, 5)
        fields(pair_of(side, 1))
        diagonal(side, 2)
        restrict_start(pair_of(side, 0))
        then(2)
        arrive(side, valid, 6, 7)
        look_up(jnp.where(side == 0, 1, 14))
        diagonal(side, 3)

    def windows(first, second):
        def tiles(value):
            return [value[:, i * LANES : (i + 1) * LANES] for i in range(CY // LANES)]

        def roll(values, steps):
            return [pltpu.roll(value, steps % LANES, 1) for value in values]

        zero = jnp.zeros((CZ, LANES), F32)
        left = [roll(tiles(first), 16 - 32 * k) for k in range(4)]
        right = [roll(tiles(second), 80 - 32 * k) for k in range(4)]
        out = []
        for i in range(CY // LANES):
            for k in range(4):
                a, b = left[k][i], right[k][i]
                if k == 0:
                    a = jnp.where(lane < 16, left[k][i - 1] if i else zero, a)
                    b = jnp.where(lane < 80, right[k][i - 1] if i else zero, b)
                if k == 3:
                    last = i + 1 == CY // LANES
                    a = jnp.where(lane < 48, a, zero if last else left[k][i + 1])
                    b = jnp.where(lane < 112, b, zero if last else right[k][i + 1])
                out.append(jnp.where(lane < 64, a, b))
        return out

    def slot(source, to_half):
        return pl.ds(1 + 2 * (source - (HALF // 2) * to_half), 2)

    def to_half(other):
        return 1 - half if other else half

    def in_halo(groups):
        return jnp.where(half == 0, s >= HALF - groups, s < HALF + groups)

    def field_copy(side, other):
        return pltpu.make_async_remote_copy(
            src_ref=fwin.at[t + SLICES * side],
            dst_ref=fbuf.at[slot(s, to_half(other))],
            send_sem=f_send.at[side, other],
            recv_sem=f_recv.at[s],
            device_id=(t, host_of(to_half(other), side)),
            device_id_type=MESH,
        )

    def field_sends(action):
        for other in range(2):
            for side in range(2):
                if other:
                    wanted = in_halo(reach(0))
                else:
                    wanted = jnp.logical_not(is_host & (side == my_side))

                @pl.when(wanted)
                def _():
                    action(field_copy(side, other))

    def coarse_row(src, row):
        outside = (is_first & (row < 2)) | (is_last & (row >= 2 + CROWS))
        c, w, e = src[row], src[row - 1], src[row + 1]
        return update(
            c, w, e,
            shifted(c, 0, CZ, 1, czi), shifted(c, 0, CZ, -1, czi),
            shifted(c, 1, CY, 1, cyi), shifted(c, 1, CY, -1, cyi),
            dc[row], ac[row], mc[row], jnp.where(outside, 0.0, 0.3), 2.0,
        )

    def from_far(row, rows):
        return jnp.where(far_side == 0, row, rows - 1 - row)

    def own_first(r):
        row = from_far(r, EXT // 2)
        rc1[row] = coarse_row(rc, row)

    def own_second(r):
        row = from_far(r, EXT // 2)
        own[row - 2] = coarse_row(rc1, row)

    def make_drift(r):
        row = from_far(r, CROWS)
        now = restrict(fine_out[2 * row] + fine_out[2 * row + 1]) - own[row]
        drift[row] = now + jnp.where(t == 0, own[row], 0.0)

    def drift_windows(r):
        q = from_far(r, CROWS // 2)
        for j, value in enumerate(windows(drift[2 * q], drift[2 * q + 1])):
            win[j, q] = value

    def own_early():
        loop(2, 7, own_first)
        loop(3, 6, own_second)

    def own_late():
        own_first(1)
        own_second(2)

    work_side(1 - far_side, True)

    def field_windows(q):
        for which, ref in enumerate((dc, ac, mc)):
            for j, value in enumerate(windows(ref[2 + 2 * q], ref[3 + 2 * q])):
                fwin[j, q, which] = value

    loop(0, CROWS // 2, field_windows)

    @pl.when(is_host)
    def _():
        fbuf[slot(s, half)] = fwin[my_window]

    greeted(known.at[1], PASSES[1])
    greet(known.at[2], PASSES[2])

    def send_fields():
        @pl.when(far_valid)
        def _():
            for index in range(len(PIECES)):
                halo_copy(index, far_to).wait_send()

        greeted(known.at[2], PASSES[2])
        field_sends(lambda copy: copy.start())
        loop(1, CROWS, make_drift)
        drift_windows(1)

    work_side(far_side, far_valid, (own_early, send_fields, own_late))
    make_drift(0)
    drift_windows(0)

    def win_copy(j, other):
        return pltpu.make_async_remote_copy(
            src_ref=win.at[j],
            dst_ref=cbuf.at[t, slot(s, to_half(other))],
            send_sem=win_send.at[j, other],
            recv_sem=win_recv.at[t, s],
            device_id=(lax.rem(j, SLICES), host_of(to_half(other), j // SLICES)),
            device_id_type=MESH,
        )

    def win_sends(action):
        sends = t < SLICES - 1

        @pl.when(sends & in_halo((17 - 2 * t) // 4))
        def _():
            for j in range(WINDOWS):
                action(win_copy(j, 1))

        @pl.when(sends & jnp.logical_not(is_host))
        def _():
            for j in range(WINDOWS):
                action(win_copy(j, 0))

        @pl.when(sends & is_host)
        def _():
            for d in range(1, WINDOWS):
                action(win_copy(lax.rem(my_window + d, WINDOWS), 0))

    win_sends(lambda copy: copy.start())

    @pl.when(is_host & (t < SLICES - 1))
    def _():
        cbuf[t, slot(s, half)] = win[my_window]

    def result_copy(link, r):
        return pltpu.make_async_remote_copy(
            src_ref=gout.at[link, r],
            dst_ref=gbuf.at[my_window],
            send_sem=g_send.at[link, r],
            recv_sem=g_recv.at[my_window],
            device_id=(link + 1, HALF * half + r),
            device_id_type=MESH,
        )

    def result_sends(link, action):
        me = s - HALF * half

        @pl.when(t != link + 1)
        def _():
            action(result_copy(link, me))

        for d in range(1, HALF):
            action(result_copy(link, lax.rem(me + d, HALF)))

    @pl.when(is_host)
    def _():
        y = 32 * my_window - 16 + lax.rem(lane, 64)
        scale = jnp.where((y >= 0) & (y < CY), 0.3, 0.0)
        edge = jnp.zeros((1, CZ, LANES), F32)
        for row in (0, PACKED + 1):
            cbuf[0, row : row + 1] = edge

        def clear_row(row):
            cw0[row] = edge[0]
            cw1[row] = edge[0]

        loop(0, PACKED + 2, clear_row)

        def source(k):
            return jnp.where(half == 0, k, SPACE - 1 - k)

        for k in range(GROUPS):
            @pl.when(source(k) != s)
            def _():
                pltpu.make_async_remote_copy(
                    src_ref=fwin.at[0], dst_ref=fbuf.at[slot(source(k), half)], send_sem=f_send.at[0, 0],
                    recv_sem=f_recv.at[source(k)], device_id=(t, s + 1), device_id_type=MESH,
                ).wait_recv()

        def wait_slice(tau):
            def wait(device):
                pltpu.make_async_remote_copy(
                    src_ref=win.at[0], dst_ref=cbuf.at[tau, slot(device, half)],
                    send_sem=win_send.at[0, 0], recv_sem=win_recv.at[tau, device],
                    device_id=(t, s + 1), device_id_type=MESH,
                ).wait_recv()

            @pl.when(t != tau)
            def _():
                wait(s)

            for d in range(1, HALF):
                wait(HALF * half + lax.rem(s + d, HALF))
            for k in range(HALF, HALF + reach(tau)):
                wait(source(k))

        def block(src, first, count):
            u = src[pl.ds(first - 1, count + 2)]
            c = u[1 : count + 1]
            crossed = pltpu.roll(u, LANES // 2, 2)
            is_left = lax.broadcasted_iota(jnp.int32, (count, CZ, LANES), 2) < LANES // 2
            zs = lax.broadcasted_iota(jnp.int32, (count, CZ, LANES), 1)
            at = pl.ds(first, count)
            return update(
                c,
                jnp.where(is_left, crossed[:count], crossed[1 : count + 1]),
                jnp.where(is_left, crossed[1 : count + 1], crossed[2:]),
                jnp.where(zs == 0, 0.0, pltpu.roll(c, 1, 1)),
                jnp.where(zs == CZ - 1, 0.0, pltpu.roll(c, CZ - 1, 1)),
                pltpu.roll(c, 1, 2), pltpu.roll(c, LANES - 1, 2),
                fbuf[at, 0], fbuf[at, 1], fbuf[at, 2], scale, 2.0,
            )

        def condense(value):
            pairs = value.reshape(HALF, 2, CZ, LANES)
            a, b = pairs[:, 0], pairs[:, 1]
            at = lax.broadcasted_iota(jnp.int32, (HALF, CZ, LANES), 2) // 32
            front = jnp.where(at == 0, pltpu.roll(a, LANES - 16, 2), pltpu.roll(a, LANES - 48, 2))
            back = jnp.where(at == 2, pltpu.roll(b, 48, 2), pltpu.roll(b, 16, 2))
            return jnp.where(at < 2, front, back)

        first_own = 1 + (PACKED - OWN_PACKED) * half

        wait_slice(0)
        for link in range(SLICES - 1):
            src = cbuf.at[0] if link == 0 else cw0
            halo = (15 - (2 * link + 1)) // 2
            first = jnp.where(half == 0, 1 + OWN_PACKED, 1 + PACKED - OWN_PACKED - halo)
            cw1[pl.ds(first_own, OWN_PACKED)] = block(src, first_own, OWN_PACKED)
            if halo:
                cw1[pl.ds(first, halo)] = block(src, first, halo)
            last = link == SLICES - 2
            if not last:
                wait_slice(link + 1)
            value = block(cw1, first_own, OWN_PACKED)
            gout[link] = condense(value)
            result_sends(link, lambda copy: copy.start())

            @pl.when(t == link + 1)
            def _():
                gbuf[my_window] = gout[link, s - HALF * half]

            if not last:
                at = pl.ds(first_own, OWN_PACKED)
                cw0[at] = value + cbuf[link + 1, at]
            halo = (15 - (2 * link + 2)) // 2
            first = jnp.where(half == 0, 1 + OWN_PACKED, 1 + PACKED - OWN_PACKED - halo)
            if halo:
                at = pl.ds(first, halo)
                cw0[at] = block(cw1, first, halo) + cbuf[link + 1, at]

    @pl.when(t == 0)
    def _():
        diff_out[...] = own[...] - own[...]

    @pl.when(t > 0)
    def _():
        def wait_result(j):
            pltpu.make_async_remote_copy(
                src_ref=gout.at[0, 0], dst_ref=gbuf.at[j], send_sem=g_send.at[0, 0],
                recv_sem=g_recv.at[j], device_id=(t, s + 1 - 2 * core), device_id_type=MESH,
            ).wait_recv()

        @pl.when(is_host)
        def _():
            for d in range(1, WINDOWS):
                wait_result(lax.rem(my_window + d, WINDOWS))

        @pl.when(jnp.logical_not(is_host))
        def _():
            for j in range(WINDOWS):
                wait_result(j)

        quarter = lane // 32

        def assemble(row):
            for i in range(CY // LANES):
                value = jnp.zeros((CZ, LANES), F32)
                for k in range(4):
                    steps = 32 * (k - row) % LANES
                    value = jnp.where(quarter == k, pltpu.roll(gbuf[4 * i + k], steps, 1), value)
                where = slice(i * LANES, (i + 1) * LANES)
                diff_out[row, :, where] = value - own[row, :, where]

        for row in range(CROWS):
            assemble(row)

    for index in range(len(PIECES)):
        halo_copy(index, 1 - far_to).wait_send()

    field_sends(lambda copy: copy.wait_send())
    win_sends(lambda copy: copy.wait_send())

    @pl.when(is_host)
    def _():
        for link in range(SLICES - 1):
            result_sends(link, lambda copy: copy.wait_send())


def correct_kernel(fine, diff, out, result, sems):
    lane = lax.broadcasted_iota(jnp.int32, (CZ, LANES), 1)
    sub = lax.broadcasted_iota(jnp.int32, (CZ, LANES), 0)

    def copy(row):
        rows = pl.ds(2 * row, 2)
        return pltpu.make_async_copy(result.at[rows], out.at[rows], sems.at[row])

    for row in range(CROWS):
        for tile in range(NY // LANES):
            index = lane // 2 + (LANES // 2) * (tile % 2)
            source = diff[row, :, (tile // 2) * LANES : (tile // 2 + 1) * LANES]
            value = jnp.take_along_axis(source, index, axis=1)
            where = slice(tile * LANES, (tile + 1) * LANES)
            for half in range(2):
                wide = jnp.take_along_axis(value, sub // 2 + 4 * half, axis=0)
                for x in range(2):
                    at = (2 * row + x, slice(8 * half, 8 * half + 8), where)
                    result[at] = fine[at] + wide
        copy(row).start()
    for row in range(CROWS):
        copy(row).wait()


def body(start_states, dispersion, soil_class, sorption_k, sorption_n):
    vmem = pl.BlockSpec(memory_space=pltpu.VMEM)
    hbm = pl.BlockSpec(memory_space=pltpu.HBM)
    dma = pltpu.SemaphoreType.DMA
    grid = (EXT, NZ, NY)
    coarse = (EXT // 2, CZ, CY)
    tile = (CZ, LANES)
    scratch = [pltpu.SMEM((12,), F32) for _ in range(2)]
    scratch += [pltpu.VMEM(grid, F32) for _ in range(4)]
    scratch += [pltpu.VMEM(grid, jnp.int32)]
    scratch += [pltpu.VMEM(grid, F32) for _ in range(2)]
    scratch += [pltpu.VMEM(coarse, F32) for _ in range(2)]
    scratch += [pltpu.VMEM((CROWS, CZ, CY), F32)]
    scratch += [pltpu.VMEM(coarse, F32) for _ in range(3)]
    scratch += [pltpu.VMEM((CROWS, CZ, CY), F32)]
    scratch += [
        pltpu.VMEM((WINDOWS, CROWS // 2) + tile, F32),
        pltpu.VMEM((WINDOWS, CROWS // 2, 3) + tile, F32),
        pltpu.VMEM((SLICES - 1, PACKED + 2) + tile, F32),
        pltpu.VMEM((PACKED + 2, 3) + tile, F32),
        pltpu.VMEM((PACKED + 2,) + tile, F32),
        pltpu.VMEM((PACKED + 2,) + tile, F32),
        pltpu.VMEM((SLICES - 1, HALF) + tile, F32),
        pltpu.VMEM((WINDOWS,) + tile, F32),
        dma((5,)),
        dma((len(PIECES), 2)),
        dma((len(PIECES), 2)),
        dma((WINDOWS, 2)),
        dma((SLICES - 1, SPACE)),
        dma((2, 2)),
        dma((SPACE,)),
        dma((SLICES - 1, HALF)),
        dma((WINDOWS,)),
        pltpu.SemaphoreType.REGULAR((3,)),
    ]
    fine, diff = pl.pallas_call(
        main_kernel,
        out_shape=(
            pltpu.VMEM((ROWS, NZ, NY), F32),
            pltpu.VMEM((CROWS, CZ, CY), F32),
        ),
        in_specs=[hbm] * 5,
        out_specs=(vmem, vmem),
        scratch_shapes=scratch,
        compiler_params=pltpu.CompilerParams(
            collective_id=0, has_side_effects=True, vmem_limit_bytes=60 * 2**20
        ),
    )(sorption_k, sorption_n, start_states[0], dispersion, soil_class)
    out = pl.pallas_call(
        correct_kernel,
        out_shape=jax.ShapeDtypeStruct((ROWS, NZ, NY), F32),
        in_specs=[vmem, vmem],
        out_specs=hbm,
        scratch_shapes=[pltpu.VMEM((ROWS, NZ, NY), F32), dma((CROWS,))],
        compiler_params=pltpu.CompilerParams(vmem_limit_bytes=20 * 2**20),
    )(fine, diff)
    return out[None]


def solution(mesh):
    in_specs = (
        P("tm", "space", None, None),
        P("space", None, None),
        P("space", None, None),
        P(),
        P(),
    )
    out_specs = P("tm", "space", None, None)
    return jax.shard_map(body, mesh=mesh, in_specs=in_specs, out_specs=out_specs, check_vma=False)
```

```python
import functools

import jax
import jax.numpy as jnp
from jax import lax
from jax.experimental import pallas as pl
from jax.experimental.pallas import tpu as pltpu
from jax.sharding import PartitionSpec as P

MESH = pl.DeviceIdType.MESH
F32 = jnp.float32

SPEED_X = 0.3
SPEED_Z = 0.2
DENSITY = 2.0
LOG2_E = 1.4426950408889634

ROWS = 8
HALO = 4
EXT = ROWS + 2 * HALO
NZ = 16
NY = 1024
CROWS = 4
CZ = 8
CY = 512
SLICES = 8
SPACE = 16
HALF = SPACE // 2
GROUPS = HALF + 4
PACKED = GROUPS * CROWS // 2
OWN_PACKED = HALF * CROWS // 2
WINDOWS = 16
LANES = 128

PIECES = (
    (0, 2, 2, 12),
    (1, 3, 1, 12),
    (2, 3, 1, 12),
    (0, 0, 2, 14),
    (1, 2, 1, 13),
    (2, 2, 1, 13),
    (1, 1, 1, 14),
    (2, 1, 1, 14),
)

PLANES = SLICES // 2
PASSES = (1, 2, 4)


def reach(tau):
    return (17 - 2 * tau) // 4


def host_of(half, side):
    return HALF // 2 + (HALF // 2) * half + 2 * side


def shifted(c, axis, size, steps, index):
    rolled = pltpu.roll(c, steps % size, axis)
    return jnp.where(index == (0 if steps > 0 else size - 1), 0.0, rolled)


def update(c, w, e, zm, zp, ym, yp, d, a, m, scale, per_h):
    lap = ((w + e) + (zm + zp)) + ((ym + yp) - 6.0 * c)
    adv = (SPEED_X * per_h) * (c - w) + (SPEED_Z * per_h) * (c - zm)
    ret = 1.0 + a * jnp.exp2(m * jnp.log(jnp.abs(c) + 0.1))
    return c + (scale * (d * lap - adv)) * pl.reciprocal(ret, approx=True)


def main_kernel(
    k_in, n_in, start, disp, soil, fine_out, diff_out,
    k_ref, n_ref, u0, u1, u2, dx, cx, ax, mx, rc, rc1, own, dc, ac, mc, drift, win, fwin,
    cbuf, fbuf, cw0, cw1, gout, gbuf,
    local_sem, halo_send, halo_recv, win_send, win_recv, f_send, f_recv, g_send, g_recv, known,
):
    t = lax.axis_index("tm")
    s = lax.axis_index("space")
    core = lax.rem(s, 2)
    half = s // HALF
    is_host = (core == 0) & (s >= host_of(0, 0)) & (s <= host_of(1, 1))
    my_side = lax.rem((s - host_of(0, 0) + SPACE) // 2, 2)
    my_window = t + SLICES * my_side
    is_first = s == 0
    is_last = s == SPACE - 1

    def clear(first):
        for ref in (u0, dx):
            ref[pl.ds(first, HALO)] = jnp.zeros((HALO, NZ, NY), F32)
        cx[pl.ds(first, HALO)] = jnp.zeros((HALO, NZ, NY), jnp.int32)

    plane = t // 2

    def greet(semaphore, distance, planes=0):
        def tell(tt, ss):
            pl.semaphore_signal(semaphore, inc=1, device_id=(tt, ss), device_id_type=MESH)

        @pl.when(s >= distance)
        def _():
            tell(t, s - distance)

        @pl.when(s < SPACE - distance)
        def _():
            tell(t, s + distance)

        if planes:
            tell(t + 1 - 2 * lax.rem(t, 2), s)
            for step in range(1, PLANES):
                there = plane + planes * step

                @pl.when((there >= 0) & (there < PLANES))
                def _():
                    tell(2 * there, s)
                    tell(2 * there + 1, s)

    def greeted(semaphore, distance, planes=0):
        count = (s >= distance).astype(jnp.int32) + (s < SPACE - distance).astype(jnp.int32)
        if planes:
            count = count + 1 + 2 * (plane if planes == 1 else PLANES - 1 - plane)
        pl.semaphore_wait(semaphore, count)

    barrier = pltpu.get_barrier_semaphore()
    greet(barrier, 1, 1)

    local = [
        pltpu.make_async_copy(src, dst.at[pl.ds(HALO, ROWS)], local_sem.at[i])
        for i, (src, dst) in enumerate(((start, u0), (disp, dx), (soil, cx)))
    ]
    local += [
        pltpu.make_async_copy(k_in, k_ref, local_sem.at[3]),
        pltpu.make_async_copy(n_in, n_ref, local_sem.at[4]),
    ]
    for copy in local:
        copy.start()

    @pl.when(is_first)
    def _():
        clear(0)

    @pl.when(is_last)
    def _():
        clear(HALO + ROWS)

    for copy in local:
        copy.wait()

    greeted(barrier, 1, 1)

    targets = (u0, dx, cx)

    def halo_copy(index, side):
        array, low, count, high = PIECES[index]
        first = jnp.where(side == 0, low, high)
        origin = jnp.where(side == 0, low + ROWS, high - ROWS)
        return pltpu.make_async_remote_copy(
            src_ref=targets[array].at[pl.ds(origin, count)],
            dst_ref=targets[array].at[pl.ds(first, count)],
            send_sem=halo_send.at[index, side],
            recv_sem=halo_recv.at[index, side],
            device_id=(t, jnp.where(side == 0, s + 1, s - 1)),
            device_id_type=MESH,
        )

    far_to = 1 - core
    far_side = core
    far_valid = jnp.logical_not(is_first | is_last)

    @pl.when(far_valid)
    def _():
        for index in range(len(PIECES)):
            halo_copy(index, far_to).start()

    for index in range(len(PIECES)):
        halo_copy(index, 1 - far_to).start()

    greet(known.at[0], PASSES[0], -1)

    lane = lax.broadcasted_iota(jnp.int32, (8, LANES), 1)
    k_table = jnp.zeros((8, LANES), F32)
    n_table = jnp.zeros((8, LANES), F32)
    for i in range(k_ref.shape[0]):
        k_table = jnp.where(lane == i, k_ref[i], k_table)
        n_table = jnp.where(lane == i, n_ref[i], n_table)
    compact = lax.rem(2 * lane, LANES)
    zi = lax.broadcasted_iota(jnp.int32, (NZ, NY), 0)
    yi = lax.broadcasted_iota(jnp.int32, (NZ, NY), 1)
    czi = lax.broadcasted_iota(jnp.int32, (CZ, CY), 0)
    cyi = lax.broadcasted_iota(jnp.int32, (CZ, CY), 1)

    def take(value, index):
        return jnp.take_along_axis(value, index, axis=1)

    def look_up(row):
        k_parts, m_parts = [], []
        for z in range(0, NZ, 8):
            k_line, m_line = [], []
            for y in range(0, NY, LANES):
                soil_now = cx[row, z : z + 8, y : y + LANES]
                k = take(k_table, soil_now)
                n = take(n_table, soil_now)
                m = n - 1.0
                ax[row, z : z + 8, y : y + LANES] = (DENSITY * k) * n
                mx[row, z : z + 8, y : y + LANES] = LOG2_E * m
                k_line.append(k)
                m_line.append(m)
            k_parts.append(jnp.concatenate(k_line, axis=1))
            m_parts.append(jnp.concatenate(m_line, axis=1))
        return jnp.concatenate(k_parts, axis=0), jnp.concatenate(m_parts, axis=0)

    sub = lax.broadcasted_iota(jnp.int32, (8, LANES), 0)
    compact_z = lax.rem(2 * sub, 8)

    def restrict(total):
        out = []
        for i in range(CY // LANES):
            halves = []
            for half in range(2):
                y = (2 * i + half) * LANES
                parts = []
                for z in range(0, NZ, 8):
                    value = total[z : z + 8, y : y + LANES]
                    value = value + pltpu.roll(value, 7, 0)
                    parts.append(jnp.take_along_axis(value, compact_z, axis=0))
                value = jnp.where(sub < 4, parts[0], parts[1])
                value = value + pltpu.roll(value, LANES - 1, 1)
                halves.append(take(value, compact))
            out.append(jnp.where(lane < LANES // 2, halves[0], halves[1]))
        return 0.125 * jnp.concatenate(out, axis=1)

    def fields(p):
        k_low, m_low = look_up(2 * p)
        k_high, m_high = look_up(2 * p + 1)
        coarse_k = restrict(k_low + k_high)
        coarse_m = restrict(m_low + m_high)
        dc[p] = restrict(dx[2 * p] + dx[2 * p + 1])
        ac[p] = (DENSITY * coarse_k) * (coarse_m + 1.0)
        mc[p] = LOG2_E * coarse_m

    def restrict_start(p):
        rc[p] = restrict(u0[2 * p] + u0[2 * p + 1])

    def fine_row(src, dst, row, shift=0):
        outside = (is_first & (row < HALO)) | (is_last & (row >= HALO + ROWS))
        c, w, e = src[row], src[row - 1], src[row + 1]
        dst[row - shift] = update(
            c, w, e,
            shifted(c, 0, NZ, 1, zi), shifted(c, 0, NZ, -1, zi),
            shifted(c, 1, NY, 1, yi), shifted(c, 1, NY, -1, yi),
            dx[row], ax[row], mx[row], jnp.where(outside, 0.0, 0.6), 1.0,
        )

    def loop(first, last, function):
        def run(i, carry):
            function(i)
            return carry

        lax.fori_loop(first, last, run, 0)

    loop(2, 6, fields)
    loop(2, 6, restrict_start)
    loop(5, 11, functools.partial(fine_row, u0, u1))
    loop(6, 10, functools.partial(fine_row, u1, u2))
    loop(7, 9, functools.partial(fine_row, u2, u1))
    greeted(known.at[0], PASSES[0], -1)
    greet(known.at[1], PASSES[1])

    def diagonal(side, d):
        for k, (src, dst) in enumerate(((u0, u1), (u1, u2), (u2, u1), (u1, fine_out))):
            low = HALO - d + k
            fine_row(src, dst, jnp.where(side == 0, low, EXT - 1 - low), HALO if k == 3 else 0)

    def arrive(side, valid, *indices):
        @pl.when(valid)
        def _():
            for index in indices:
                halo_copy(index, side).wait_recv()

    def pair_of(side, p):
        return jnp.where(side == 0, p, EXT // 2 - 1 - p)

    def work_side(side, valid, after=(None, None, None)):
        def then(index):
            if after[index] is not None:
                after[index]()

        arrive(side, valid, 0)
        diagonal(side, 0)
        restrict_start(pair_of(side, 1))
        then(0)
        arrive(side, valid, 1, 2)
        look_up(jnp.where(side == 0, 3, 12))
        diagonal(side, 1)
        then(1)
        arrive(side, valid, 3, 4, 5)
        fields(pair_of(side, 1))
        diagonal(side, 2)
        restrict_start(pair_of(side, 0))
        then(2)
        arrive(side, valid, 6, 7)
        look_up(jnp.where(side == 0, 1, 14))
        diagonal(side, 3)

    def windows(first, second):
        def tiles(value):
            return [value[:, i * LANES : (i + 1) * LANES] for i in range(CY // LANES)]

        def roll(values, steps):
            return [pltpu.roll(value, steps % LANES, 1) for value in values]

        zero = jnp.zeros((CZ, LANES), F32)
        left = [roll(tiles(first), 16 - 32 * k) for k in range(4)]
        right = [roll(tiles(second), 80 - 32 * k) for k in range(4)]
        out = []
        for i in range(CY // LANES):
            for k in range(4):
                a, b = left[k][i], right[k][i]
                if k == 0:
                    a = jnp.where(lane < 16, left[k][i - 1] if i else zero, a)
                    b = jnp.where(lane < 80, right[k][i - 1] if i else zero, b)
                if k == 3:
                    last = i + 1 == CY // LANES
                    a = jnp.where(lane < 48, a, zero if last else left[k][i + 1])
                    b = jnp.where(lane < 112, b, zero if last else right[k][i + 1])
                out.append(jnp.where(lane < 64, a, b))
        return out

    def slot(source, to_half):
        return pl.ds(1 + 2 * (source - (HALF // 2) * to_half), 2)

    def to_half(other):
        return 1 - half if other else half

    def in_halo(groups):
        return jnp.where(half == 0, s >= HALF - groups, s < HALF + groups)

    def field_copy(side, other):
        return pltpu.make_async_remote_copy(
            src_ref=fwin.at[t + SLICES * side],
            dst_ref=fbuf.at[slot(s, to_half(other))],
            send_sem=f_send.at[side, other],
            recv_sem=f_recv.at[s],
            device_id=(t, host_of(to_half(other), side)),
            device_id_type=MESH,
        )

    def field_sends(action):
        for other in range(2):
            for side in range(2):
                if other:
                    wanted = in_halo(reach(0))
                else:
                    wanted = jnp.logical_not(is_host & (side == my_side))

                @pl.when(wanted)
                def _():
                    action(field_copy(side, other))

    def coarse_row(src, row):
        outside = (is_first & (row < 2)) | (is_last & (row >= 2 + CROWS))
        c, w, e = src[row], src[row - 1], src[row + 1]
        return update(
            c, w, e,
            shifted(c, 0, CZ, 1, czi), shifted(c, 0, CZ, -1, czi),
            shifted(c, 1, CY, 1, cyi), shifted(c, 1, CY, -1, cyi),
            dc[row], ac[row], mc[row], jnp.where(outside, 0.0, 0.3), 2.0,
        )

    def from_far(row, rows):
        return jnp.where(far_side == 0, row, rows - 1 - row)

    def own_first(r):
        row = from_far(r, EXT // 2)
        rc1[row] = coarse_row(rc, row)

    def own_second(r):
        row = from_far(r, EXT // 2)
        own[row - 2] = coarse_row(rc1, row)

    def make_drift(r):
        row = from_far(r, CROWS)
        now = restrict(fine_out[2 * row] + fine_out[2 * row + 1]) - own[row]
        drift[row] = now + jnp.where(t == 0, own[row], 0.0)

    def drift_windows(r):
        q = from_far(r, CROWS // 2)
        for j, value in enumerate(windows(drift[2 * q], drift[2 * q + 1])):
            win[j, q] = value

    def own_early():
        loop(2, 7, own_first)
        loop(3, 6, own_second)

    def own_late():
        own_first(1)
        own_second(2)

    work_side(1 - far_side, True)

    def field_windows(q):
        for which, ref in enumerate((dc, ac, mc)):
            for j, value in enumerate(windows(ref[2 + 2 * q], ref[3 + 2 * q])):
                fwin[j, q, which] = value

    loop(0, CROWS // 2, field_windows)

    @pl.when(is_host)
    def _():
        fbuf[slot(s, half)] = fwin[my_window]

    greeted(known.at[1], PASSES[1])
    greet(known.at[2], PASSES[2])

    def send_fields():
        @pl.when(far_valid)
        def _():
            for index in range(len(PIECES)):
                halo_copy(index, far_to).wait_send()

        greeted(known.at[2], PASSES[2])
        field_sends(lambda copy: copy.start())
        loop(1, CROWS, make_drift)
        drift_windows(1)

    work_side(far_side, far_valid, (own_early, send_fields, own_late))
    make_drift(0)
    drift_windows(0)

    def win_copy(j, other):
        return pltpu.make_async_remote_copy(
            src_ref=win.at[j],
            dst_ref=cbuf.at[t, slot(s, to_half(other))],
            send_sem=win_send.at[j, other],
            recv_sem=win_recv.at[t, s],
            device_id=(lax.rem(j, SLICES), host_of(to_half(other), j // SLICES)),
            device_id_type=MESH,
        )

    def win_sends(action):
        sends = t < SLICES - 1

        @pl.when(sends & in_halo((17 - 2 * t) // 4))
        def _():
            for j in range(WINDOWS):
                action(win_copy(j, 1))

        @pl.when(sends & jnp.logical_not(is_host))
        def _():
            for j in range(WINDOWS):
                action(win_copy(j, 0))

        @pl.when(sends & is_host)
        def _():
            for d in range(1, WINDOWS):
                action(win_copy(lax.rem(my_window + d, WINDOWS), 0))

    win_sends(lambda copy: copy.start())

    @pl.when(is_host & (t < SLICES - 1))
    def _():
        cbuf[t, slot(s, half)] = win[my_window]

    def result_copy(link, r):
        return pltpu.make_async_remote_copy(
            src_ref=gout.at[link, r],
            dst_ref=gbuf.at[my_window],
            send_sem=g_send.at[link, r],
            recv_sem=g_recv.at[my_window],
            device_id=(link + 1, HALF * half + r),
            device_id_type=MESH,
        )

    def result_sends(link, action):
        me = s - HALF * half

        @pl.when(t != link + 1)
        def _():
            action(result_copy(link, me))

        for d in range(1, HALF):
            action(result_copy(link, lax.rem(me + d, HALF)))

    @pl.when(is_host)
    def _():
        y = 32 * my_window - 16 + lax.rem(lane, 64)
        scale = jnp.where((y >= 0) & (y < CY), 0.3, 0.0)
        edge = jnp.zeros((1, CZ, LANES), F32)
        for row in (0, PACKED + 1):
            cbuf[0, row : row + 1] = edge

        def clear_row(row):
            cw0[row] = edge[0]
            cw1[row] = edge[0]

        loop(0, PACKED + 2, clear_row)

        def source(k):
            return jnp.where(half == 0, k, SPACE - 1 - k)

        for k in range(GROUPS):
            @pl.when(source(k) != s)
            def _():
                pltpu.make_async_remote_copy(
                    src_ref=fwin.at[0], dst_ref=fbuf.at[slot(source(k), half)], send_sem=f_send.at[0, 0],
                    recv_sem=f_recv.at[source(k)], device_id=(t, s + 1), device_id_type=MESH,
                ).wait_recv()

        def wait_slice(tau):
            def wait(device):
                pltpu.make_async_remote_copy(
                    src_ref=win.at[0], dst_ref=cbuf.at[tau, slot(device, half)],
                    send_sem=win_send.at[0, 0], recv_sem=win_recv.at[tau, device],
                    device_id=(t, s + 1), device_id_type=MESH,
                ).wait_recv()

            @pl.when(t != tau)
            def _():
                wait(s)

            for d in range(1, HALF):
                wait(HALF * half + lax.rem(s + d, HALF))
            for k in range(HALF, HALF + reach(tau)):
                wait(source(k))

        def block(src, first, count):
            u = src[pl.ds(first - 1, count + 2)]
            c = u[1 : count + 1]
            crossed = pltpu.roll(u, LANES // 2, 2)
            is_left = lax.broadcasted_iota(jnp.int32, (count, CZ, LANES), 2) < LANES // 2
            zs = lax.broadcasted_iota(jnp.int32, (count, CZ, LANES), 1)
            at = pl.ds(first, count)
            return update(
                c,
                jnp.where(is_left, crossed[:count], crossed[1 : count + 1]),
                jnp.where(is_left, crossed[1 : count + 1], crossed[2:]),
                jnp.where(zs == 0, 0.0, pltpu.roll(c, 1, 1)),
                jnp.where(zs == CZ - 1, 0.0, pltpu.roll(c, CZ - 1, 1)),
                pltpu.roll(c, 1, 2), pltpu.roll(c, LANES - 1, 2),
                fbuf[at, 0], fbuf[at, 1], fbuf[at, 2], scale, 2.0,
            )

        def condense(value):
            pairs = value.reshape(HALF, 2, CZ, LANES)
            a, b = pairs[:, 0], pairs[:, 1]
            at = lax.broadcasted_iota(jnp.int32, (HALF, CZ, LANES), 2) // 32
            front = jnp.where(at == 0, pltpu.roll(a, LANES - 16, 2), pltpu.roll(a, LANES - 48, 2))
            back = jnp.where(at == 2, pltpu.roll(b, 48, 2), pltpu.roll(b, 16, 2))
            return jnp.where(at < 2, front, back)

        first_own = 1 + (PACKED - OWN_PACKED) * half

        wait_slice(0)
        for link in range(SLICES - 1):
            src = cbuf.at[0] if link == 0 else cw0
            halo = (15 - (2 * link + 1)) // 2
            first = jnp.where(half == 0, 1 + OWN_PACKED, 1 + PACKED - OWN_PACKED - halo)
            cw1[pl.ds(first_own, OWN_PACKED)] = block(src, first_own, OWN_PACKED)
            if halo:
                cw1[pl.ds(first, halo)] = block(src, first, halo)
            last = link == SLICES - 2
            if not last:
                wait_slice(link + 1)
            value = block(cw1, first_own, OWN_PACKED)
            gout[link] = condense(value)
            result_sends(link, lambda copy: copy.start())

            @pl.when(t == link + 1)
            def _():
                gbuf[my_window] = gout[link, s - HALF * half]

            if not last:
                at = pl.ds(first_own, OWN_PACKED)
                cw0[at] = value + cbuf[link + 1, at]
            halo = (15 - (2 * link + 2)) // 2
            first = jnp.where(half == 0, 1 + OWN_PACKED, 1 + PACKED - OWN_PACKED - halo)
            if halo:
                at = pl.ds(first, halo)
                cw0[at] = block(cw1, first, halo) + cbuf[link + 1, at]

    @pl.when(t == 0)
    def _():
        diff_out[...] = own[...] - own[...]

    @pl.when(t > 0)
    def _():
        def wait_result(j):
            pltpu.make_async_remote_copy(
                src_ref=gout.at[0, 0], dst_ref=gbuf.at[j], send_sem=g_send.at[0, 0],
                recv_sem=g_recv.at[j], device_id=(t, s + 1 - 2 * core), device_id_type=MESH,
            ).wait_recv()

        @pl.when(is_host)
        def _():
            for d in range(1, WINDOWS):
                wait_result(lax.rem(my_window + d, WINDOWS))

        @pl.when(jnp.logical_not(is_host))
        def _():
            for j in range(WINDOWS):
                wait_result(j)

        quarter = lane // 32

        def assemble(row):
            for i in range(CY // LANES):
                value = jnp.zeros((CZ, LANES), F32)
                for k in range(4):
                    steps = 32 * (k - row) % LANES
                    value = jnp.where(quarter == k, pltpu.roll(gbuf[4 * i + k], steps, 1), value)
                where = slice(i * LANES, (i + 1) * LANES)
                diff_out[row, :, where] = value - own[row, :, where]

        for row in range(CROWS):
            assemble(row)

    for index in range(len(PIECES)):
        halo_copy(index, 1 - far_to).wait_send()

    field_sends(lambda copy: copy.wait_send())
    win_sends(lambda copy: copy.wait_send())

    @pl.when(is_host)
    def _():
        for link in range(SLICES - 1):
            result_sends(link, lambda copy: copy.wait_send())


def correct_kernel(fine, diff, out, result, sems):
    lane = lax.broadcasted_iota(jnp.int32, (CZ, LANES), 1)
    sub = lax.broadcasted_iota(jnp.int32, (CZ, LANES), 0)

    def copy(row):
        rows = pl.ds(2 * row, 2)
        return pltpu.make_async_copy(result.at[rows], out.at[rows], sems.at[row])

    for row in range(CROWS):
        for tile in range(NY // LANES):
            index = lane // 2 + (LANES // 2) * (tile % 2)
            source = diff[row, :, (tile // 2) * LANES : (tile // 2 + 1) * LANES]
            value = jnp.take_along_axis(source, index, axis=1)
            where = slice(tile * LANES, (tile + 1) * LANES)
            for half in range(2):
                wide = jnp.take_along_axis(value, sub // 2 + 4 * half, axis=0)
                for x in range(2):
                    at = (2 * row + x, slice(8 * half, 8 * half + 8), where)
                    result[at] = fine[at] + wide
        copy(row).start()
    for row in range(CROWS):
        copy(row).wait()


def body(start_states, dispersion, soil_class, sorption_k, sorption_n):
    vmem = pl.BlockSpec(memory_space=pltpu.VMEM)
    hbm = pl.BlockSpec(memory_space=pltpu.HBM)
    dma = pltpu.SemaphoreType.DMA
    grid = (EXT, NZ, NY)
    coarse = (EXT // 2, CZ, CY)
    tile = (CZ, LANES)
    scratch = [pltpu.SMEM((12,), F32) for _ in range(2)]
    scratch += [pltpu.VMEM(grid, F32) for _ in range(4)]
    scratch += [pltpu.VMEM(grid, jnp.int32)]
    scratch += [pltpu.VMEM(grid, F32) for _ in range(2)]
    scratch += [pltpu.VMEM(coarse, F32) for _ in range(2)]
    scratch += [pltpu.VMEM((CROWS, CZ, CY), F32)]
    scratch += [pltpu.VMEM(coarse, F32) for _ in range(3)]
    scratch += [pltpu.VMEM((CROWS, CZ, CY), F32)]
    scratch += [
        pltpu.VMEM((WINDOWS, CROWS // 2) + tile, F32),
        pltpu.VMEM((WINDOWS, CROWS // 2, 3) + tile, F32),
        pltpu.VMEM((SLICES - 1, PACKED + 2) + tile, F32),
        pltpu.VMEM((PACKED + 2, 3) + tile, F32),
        pltpu.VMEM((PACKED + 2,) + tile, F32),
        pltpu.VMEM((PACKED + 2,) + tile, F32),
        pltpu.VMEM((SLICES - 1, HALF) + tile, F32),
        pltpu.VMEM((WINDOWS,) + tile, F32),
        dma((5,)),
        dma((len(PIECES), 2)),
        dma((len(PIECES), 2)),
        dma((WINDOWS, 2)),
        dma((SLICES - 1, SPACE)),
        dma((2, 2)),
        dma((SPACE,)),
        dma((SLICES - 1, HALF)),
        dma((WINDOWS,)),
        pltpu.SemaphoreType.REGULAR((3,)),
    ]
    fine, diff = pl.pallas_call(
        main_kernel,
        out_shape=(
            pltpu.VMEM((ROWS, NZ, NY), F32),
            pltpu.VMEM((CROWS, CZ, CY), F32),
        ),
        in_specs=[hbm] * 5,
        out_specs=(vmem, vmem),
        scratch_shapes=scratch,
        compiler_params=pltpu.CompilerParams(
            collective_id=0, has_side_effects=True, vmem_limit_bytes=60 * 2**20
        ),
    )(sorption_k, sorption_n, start_states[0], dispersion, soil_class)
    out = pl.pallas_call(
        correct_kernel,
        out_shape=jax.ShapeDtypeStruct((ROWS, NZ, NY), F32),
        in_specs=[vmem, vmem],
        out_specs=hbm,
        scratch_shapes=[pltpu.VMEM((ROWS, NZ, NY), F32), dma((CROWS,))],
        compiler_params=pltpu.CompilerParams(vmem_limit_bytes=20 * 2**20),
    )(fine, diff)
    return out[None]


def solution(mesh):
    in_specs = (
        P("tm", "space", None, None),
        P("space", None, None),
        P("space", None, None),
        P(),
        P(),
    )
    out_specs = P("tm", "space", None, None)
    return jax.shard_map(body, mesh=mesh, in_specs=in_specs, out_specs=out_specs, check_vma=False)
```
